128 devices in a mesh: radon: 8 (over y_lo, z), freq: 16 (over y_hi, x, core).
Axes of the slice: x: 4, y: 4 (y_hi: 2, y_lo: 2; y = y_hi * 2 + y_lo), z: 4, core: 2. Of those that a mesh axis runs over, the one named last changes fastest.
Arguments:
- shot_traces: float32 [384, 1024, 1024], P('radon', 'freq'), may hold values from -6 to 6
- radon_weights: float32 [2, 1024, 256], P(None, 'freq'), may hold values from -0.1875 to 0.1875
- source_weights: float32 [384, 256], replicated, may hold values from -0.01953125 to 0.01953125
- line_index: int32 [384], replicated, may hold values from 0 to 1, as said below
- panel_index: int32 [384], replicated, may hold values from 0 to 1, as said below
Outputs:
- multiples: float32 [256, 2, 384, 256], P('freq', None, 'radon')
The draws below stay inside these ranges and needn't reach their ends.
Inputs may be any that keep to these rules, and one draw needn't show every extreme that they name: `line_index`: in every aligned block of 48 shots, each geometry holds exactly 24 shots. `panel_index`: in every aligned block of 48 shots, each panel holds exactly 24 shots.
All inputs are finite; a program needn't handle non-finite values.
Results may differ from the reference program's by a relative error of at most 0.0001.
Values sent between devices are 32-bit elements; how exact they have to be, the bound alone decides.
No kernel may reach another device: no remote copies, remote signals or barrier semaphores. Data moves between devices by JAX's collectives and lax.ppermute only.
A program may use at most 128 MiB of HBM per device.

```python
import jax
import jax.numpy as jnp
from jax import lax

X = 1024
NT = 1024
NF = 256
P_SIZE = 256
L = 2
K = 2
SHOT_DEV = 48
SHOTS = 384


def balanced_labels(key, count):
    blocks = SHOTS // SHOT_DEV
    base = jnp.arange(SHOT_DEV, dtype=jnp.int32) % count
    keys = jax.random.split(key, blocks)
    shuffled = jax.vmap(lambda one_key: jax.random.permutation(one_key, base))(keys)
    return shuffled.reshape(SHOTS).astype(jnp.int32)


def draw_line_index(key, part):
    key = jax.random.fold_in(key, 11)
    return balanced_labels(key, L)


def draw_panel_index(key, part):
    key = jax.random.fold_in(key, 23)
    return balanced_labels(key, K)


def shard_levels(key, extent, cuts, least, largest):
    gain = 1.0
    for position, parts in cuts:
        heights = jax.random.uniform(jax.random.fold_in(jax.random.fold_in(key, 6), position), (parts,), jnp.float32, least / len(cuts), largest / len(cuts))
        gain = gain * jnp.repeat(jnp.exp(heights), extent[position] // parts).reshape((-1,) + (1,) * (len(extent) - 1 - position))
    return gain


def normal_values(stream_key, shape, deviation, most, pieces=(), kind=jnp.bfloat16):
    level = shard_levels(stream_key, shape, pieces, -0.22, 0.18) if pieces else 1.0
    entries = jax.random.normal(stream_key, shape, jnp.float32) * deviation * level
    return jnp.minimum(jnp.maximum(entries, -most), most).astype(kind)


def setup_inputs(seed: int = 0) -> dict:
    seeds = jax.random.split(jax.random.key(seed), 6)
    return {
        "shot_traces": normal_values(seeds[0], (SHOTS, X, NT), 1.0, 6.0, ((0, 8), (1, 16)), jnp.float32),
        "radon_weights": normal_values(seeds[1], (L, X, P_SIZE), X ** -0.5, 0.1875, ((1, 16),), jnp.float32),
        "source_weights": normal_values(seeds[2], (SHOTS, P_SIZE), (SHOTS * P_SIZE) ** -0.5, 0.01953125, (), jnp.float32),
        "line_index": draw_line_index(jax.random.fold_in(seeds[5], 71), 0),
        "panel_index": draw_panel_index(jax.random.fold_in(seeds[5], 71), 0),
    }


highest = lax.Precision.HIGHEST


def reference(shot_traces, radon_weights, source_weights, line_index, panel_index):
    def one_shot(operands):
        traces, line_value = operands
        spectrum = jnp.fft.rfft(traces, axis=-1)[:, :NF] * (NT ** -0.5)
        stacked = jnp.stack([jnp.real(spectrum), jnp.imag(spectrum)]).astype(jnp.float32)
        weights = lax.dynamic_index_in_dim(radon_weights, line_value, 0, keepdims=False)
        return jnp.einsum('xp,cxf->fcp', weights, stacked, precision=highest)

    gathers = lax.map(one_shot, (shot_traces, line_index))
    gathers = jnp.transpose(gathers, (1, 2, 0, 3))
    onehot = (panel_index[:, None] == jnp.arange(K, dtype=jnp.int32)[None, :]).astype(jnp.float32)
    masked = source_weights[:, None, :] * onehot[:, :, None]

    def one_freq(slab):
        panels = jnp.einsum('skq,csp->kcqp', masked, slab, precision=highest)
        real_part = jnp.einsum('sq,kqp->ksp', slab[0], panels[:, 0], precision=highest) - jnp.einsum('sq,kqp->ksp', slab[1], panels[:, 1], precision=highest)
        imag_part = jnp.einsum('sq,kqp->ksp', slab[0], panels[:, 1], precision=highest) + jnp.einsum('sq,kqp->ksp', slab[1], panels[:, 0], precision=highest)
        chosen_real = jnp.einsum('sk,ksp->sp', onehot, real_part, precision=highest)
        chosen_imag = jnp.einsum('sk,ksp->sp', onehot, imag_part, precision=highest)
        return jnp.stack([chosen_real, chosen_imag])

    return lax.map(one_freq, gathers)
```

```python
import functools

import jax
import jax.numpy as jnp
import ml_dtypes
import numpy as np
from jax import lax
from jax.experimental import pallas as pl
from jax.experimental.pallas import tpu as pltpu
from jax.sharding import PartitionSpec as P

NT = 1024
NF = 256
P_SIZE = 256
L = 2
K = 2
HALF = NT // 2
LANES = 128
BINS = 2
ROWS = 8
SPREAD = ROWS // (2 * BINS)


def split(x):
    hi = x.astype(jnp.bfloat16)
    lo = (x - hi.astype(jnp.float32)).astype(jnp.bfloat16)
    return hi, lo


def dot3(a, b, dims=(((1,), (0,)), ((), ()))):
    dot = functools.partial(
        lax.dot_general, dimension_numbers=dims, preferred_element_type=jnp.float32
    )
    return dot(a[0], b[0]) + (dot(a[0], b[1]) + dot(a[1], b[0]))


def dft_tables(radon_size, freq_size):
    band = NF // freq_size
    device = np.arange(radon_size * freq_size)
    rows = []
    for parity in range(BINS):
        bins = band * (device % freq_size) + BINS * (device // freq_size) + parity
        phase = (bins[:, None] * np.arange(HALF)[None, :] % NT) * (2.0 * np.pi / NT)
        rows += [np.cos(phase), -np.sin(phase)]
    table = (np.concatenate(rows) * NT ** (-0.5)).astype(np.float32)
    hi = table.astype(ml_dtypes.bfloat16)
    lo = (table - hi.astype(np.float32)).astype(ml_dtypes.bfloat16)
    return np.stack([hi, lo])


def dft_kernel(devices, *refs):
    count = 4 * SPREAD
    x_refs, (table_ref, out_ref), tiles = refs[:count], refs[count : count + 2], refs[count + 2 :]
    for sh in range(SPREAD):
        rows = jnp.concatenate([x_refs[SPREAD * i + sh][0] for i in range(4)], axis=0)
        head, tail = rows[:, :HALF], rows[:, HALF:]
        for parity in range(BINS):
            folded = split(head - tail if parity else head + tail)
            at = slice(2 * parity * devices, 2 * (parity + 1) * devices)
            spectrum = dot3(
                (table_ref[0, at], table_ref[1, at]), folded, (((1,), (1,)), ((), ()))
            )
            for part in range(2):
                row = (sh * BINS + parity) * 2 + part
                for h, tile in enumerate(tiles):
                    tile[pl.ds(row, devices, stride=ROWS), :] = spectrum[
                        part * devices : (part + 1) * devices, h * LANES : (h + 1) * LANES
                    ]
    for h, tile in enumerate(tiles):
        out_ref[:, h * LANES : (h + 1) * LANES] = tile[...]


def dft(traces, radon_size, freq_size):
    shots, channels, _ = traces.shape
    devices = radon_size * freq_size
    step = 4 * SPREAD
    lanes = shots // SPREAD * channels
    table = jnp.asarray(dft_tables(radon_size, freq_size))
    return pl.pallas_call(
        functools.partial(dft_kernel, devices),
        grid=(shots // step,),
        in_specs=[
            pl.BlockSpec((1, channels, NT), lambda g, n=n: (g * step + n, 0, 0))
            for n in range(step)
        ]
        + [pl.BlockSpec(table.shape, lambda g: (0, 0, 0))],
        out_specs=pl.BlockSpec((devices * ROWS, 4 * channels), lambda g: (0, g)),
        out_shape=jax.ShapeDtypeStruct((devices * ROWS, lanes), jnp.float32),
        scratch_shapes=[pltpu.VMEM((devices * ROWS, LANES), jnp.float32)]
        * (4 * channels // LANES),
        compiler_params=pltpu.CompilerParams(vmem_limit_bytes=48 * 2**20),
        cost_estimate=pl.CostEstimate(
            flops=3 * table.size * shots * channels,
            bytes_accessed=4 * (traces.size + devices * ROWS * lanes),
            transcendentals=0,
        ),
    )(*[traces] * step, table)


def weights_kernel(w_ref, hi_ref, lo_ref):
    channels = w_ref.shape[2]
    for j in range(w_ref.shape[0]):
        for line in range(L):
            at = (pl.ds(j * channels, channels), pl.ds(line * P_SIZE, P_SIZE))
            hi_ref[at], lo_ref[at] = split(w_ref[j, line])


def split_weights(weights):
    freq_size, _, channels, _ = weights.shape
    out = jax.ShapeDtypeStruct((freq_size * channels, L * P_SIZE), jnp.bfloat16)
    return pl.pallas_call(
        weights_kernel,
        out_shape=(out, out),
        compiler_params=pltpu.CompilerParams(vmem_limit_bytes=48 * 2**20),
        cost_estimate=pl.CostEstimate(
            flops=10**11, bytes_accessed=8 * weights.size, transcendentals=0
        ),
    )(weights)


def panel_kernel(freq_size, count, *refs):
    rec_refs = refs[:count]
    (hi_ref, lo_ref, line_ref, src_ref, panel_ref, out_ref, a_hi, a_lo) = refs[count : count + 8]
    gathers = refs[count + 8 :]
    step = pl.program_id(0)
    steps = pl.num_programs(0)
    channels = hi_ref.shape[0] // freq_size
    slots = rec_refs[0].shape[1] // channels

    low = lax.broadcasted_iota(jnp.int32, (ROWS, 2 * channels), 1) < channels
    for r, rec_ref in enumerate(rec_refs):
        for t in range(slots // 2):
            firsts, seconds = [], []
            for pair in range(freq_size // 2):
                at = pl.ds(t * 2 * channels, 2 * channels)
                a = rec_ref[pl.ds(2 * pair * ROWS, ROWS), at]
                b = rec_ref[pl.ds((2 * pair + 1) * ROWS, ROWS), at]
                firsts.append(jnp.where(low, a, pltpu.roll(b, channels, 1)))
                seconds.append(jnp.where(low, pltpu.roll(a, channels, 1), b))
            both = jnp.concatenate(
                [jnp.concatenate(firsts, axis=1), jnp.concatenate(seconds, axis=1)], axis=0
            )
            at = pl.ds((r * slots + 2 * t) * ROWS, 2 * ROWS)
            a_hi[at, :], a_lo[at, :] = split(both)
    lines = dot3((a_hi[...], a_lo[...]), (hi_ref[...], lo_ref[...]))
    rows = count * slots * ROWS
    chosen = jnp.where(line_ref[...] == 0, lines[:, :P_SIZE], lines[:, P_SIZE:])
    for h, tile in enumerate(gathers):
        tile[pl.ds(pl.multiple_of(step * rows, rows), rows), :] = chosen[
            :, h * LANES : (h + 1) * LANES
        ]

    @pl.when(step == steps - 1)
    def _():
        shots = src_ref.shape[1]
        own = shots // out_ref.shape[0]
        source = split(src_ref[...])
        first = panel_ref[...] == 0
        for n in range(BINS):
            parts, panels = [], []
            for part in range(2):
                at = pl.ds(2 * n + part, shots, stride=2 * BINS)
                rows = jnp.concatenate([tile[at, :] for tile in gathers], axis=1)
                parts.append(split(rows))
                panels.append(dot3(source, parts[part]))
            chosen = None
            for k in range(K):
                at = slice(k * P_SIZE, (k + 1) * P_SIZE)
                real, imag = split(panels[0][at]), split(panels[1][at])
                out_real = dot3(parts[0], real) - dot3(parts[1], imag)
                out_imag = dot3(parts[0], imag) + dot3(parts[1], real)
                if k == 0:
                    chosen = (out_real, out_imag)
                else:
                    chosen = (
                        jnp.where(first, chosen[0], out_real),
                        jnp.where(first, chosen[1], out_imag),
                    )
            for part in range(2):
                for r in range(out_ref.shape[0]):
                    out_ref[r, n, part] = chosen[part][r * own : (r + 1) * own]


def panel_products(received, weights, lines, sources, panel_rows, freq_size, radon_size):
    lanes = received.shape[1]
    depth, columns = weights[0].shape
    channels = depth // freq_size
    slots = lanes // channels
    grid = 4
    count = radon_size // grid
    rows = count * slots * ROWS
    shots = sources.shape[1]
    out = (radon_size, BINS, 2, shots // radon_size, P_SIZE)
    return pl.pallas_call(
        functools.partial(panel_kernel, freq_size, count),
        grid=(grid,),
        in_specs=[
            pl.BlockSpec((freq_size * ROWS, lanes), lambda r, n=n: (count * r + n, 0))
            for n in range(count)
        ]
        + [
            pl.BlockSpec((depth, columns), lambda r: (0, 0)),
            pl.BlockSpec((depth, columns), lambda r: (0, 0)),
            pl.BlockSpec((rows, 1), lambda r: (r, 0)),
            pl.BlockSpec(sources.shape, lambda r: (0, 0)),
            pl.BlockSpec((shots, 1), lambda r: (0, 0)),
        ],
        out_specs=pl.BlockSpec(out, lambda r: (0, 0, 0, 0, 0)),
        out_shape=jax.ShapeDtypeStruct(out, jnp.float32),
        scratch_shapes=[pltpu.VMEM((rows, depth), jnp.bfloat16)] * 2
        + [pltpu.VMEM((grid * rows, LANES), jnp.float32)] * (P_SIZE // LANES),
        compiler_params=pltpu.CompilerParams(vmem_limit_bytes=48 * 2**20),
        cost_estimate=pl.CostEstimate(
            flops=6 * grid * rows * depth * columns,
            bytes_accessed=4 * received.size,
            transcendentals=0,
        ),
    )(*[received] * count, *weights, lines, sources, panel_rows)


def shards(shot_traces, radon_weights, source_weights, line_index, panel_index):
    shot_rows = shot_traces.shape[0]
    freq_size = lax.axis_size("freq")
    radon_size = lax.axis_size("radon")

    weights = lax.all_gather(radon_weights, "freq", axis=0)
    weights = split_weights(weights)
    messages = dft(shot_traces, radon_size, freq_size)
    received = lax.all_to_all(messages, ("radon", "freq"), 0, 0, tiled=True)

    lines = jnp.repeat(line_index, 2 * BINS)[:, None]
    onehot = panel_index[None, :] == jnp.arange(K, dtype=jnp.int32)[:, None]
    sources = jnp.where(onehot[:, None, :], source_weights.T[None], 0.0).reshape(K * P_SIZE, -1)

    products = panel_products(
        received, weights, lines, sources, panel_index[:, None], freq_size, radon_size
    )
    result = lax.all_to_all(products, "radon", 0, 0, tiled=True)
    return result.reshape(BINS * radon_size, 2, shot_rows, P_SIZE)


def solution(mesh):
    placed = (P("radon", "freq", None), P(None, "freq", None), P(), P(), P())
    return jax.shard_map(
        shards,
        mesh=mesh,
        in_specs=placed,
        out_specs=P("freq", None, "radon", None),
        check_vma=False,
    )
```

```python
import functools

import jax
import jax.numpy as jnp
import ml_dtypes
import numpy as np
from jax import lax
from jax.experimental import pallas as pl
from jax.experimental.pallas import tpu as pltpu
from jax.sharding import PartitionSpec as P

NT = 1024
NF = 256
P_SIZE = 256
L = 2
K = 2
HALF = NT // 2
LANES = 128
BINS = 2
ROWS = 8
SPREAD = ROWS // (2 * BINS)


def split(x):
    hi = x.astype(jnp.bfloat16)
    lo = (x - hi.astype(jnp.float32)).astype(jnp.bfloat16)
    return hi, lo


def dot3(a, b, dims=(((1,), (0,)), ((), ()))):
    dot = functools.partial(
        lax.dot_general, dimension_numbers=dims, preferred_element_type=jnp.float32
    )
    return dot(a[0], b[0]) + (dot(a[0], b[1]) + dot(a[1], b[0]))


def dft_tables(radon_size, freq_size):
    band = NF // freq_size
    device = np.arange(radon_size * freq_size)
    rows = []
    for parity in range(BINS):
        bins = band * (device % freq_size) + BINS * (device // freq_size) + parity
        phase = (bins[:, None] * np.arange(HALF)[None, :] % NT) * (2.0 * np.pi / NT)
        rows += [np.cos(phase), -np.sin(phase)]
    table = (np.concatenate(rows) * NT ** (-0.5)).astype(np.float32)
    hi = table.astype(ml_dtypes.bfloat16)
    lo = (table - hi.astype(np.float32)).astype(ml_dtypes.bfloat16)
    return np.stack([hi, lo])


def dft_kernel(devices, *refs):
    x_refs, (table_ref, out_ref) = refs[:-2], refs[-2:]
    groups = len(x_refs) // SPREAD
    width = groups * x_refs[0].shape[1] // LANES
    message = out_ref.shape[0] // devices
    for sh in range(SPREAD):
        rows = jnp.concatenate([x_refs[SPREAD * i + sh][0] for i in range(groups)], axis=0)
        head, tail = rows[:, :HALF], rows[:, HALF:]
        for parity in range(BINS):
            folded = split(head - tail if parity else head + tail)
            at = slice(2 * parity * devices, 2 * (parity + 1) * devices)
            spectrum = dot3(
                (table_ref[0, at], table_ref[1, at]), folded, (((1,), (1,)), ((), ()))
            )
            for part in range(2):
                for h in range(width):
                    tile = pl.program_id(0) * width + h
                    row = tile * ROWS + (sh * BINS + parity) * 2 + part
                    out_ref[pl.ds(row, devices, stride=message), :] = spectrum[
                        part * devices : (part + 1) * devices, h * LANES : (h + 1) * LANES
                    ]


def dft(traces, radon_size, freq_size):
    shots, channels, _ = traces.shape
    devices = radon_size * freq_size
    step = 4 * SPREAD
    rows = devices * ROWS * (shots // SPREAD) * channels // LANES
    table = jnp.asarray(dft_tables(radon_size, freq_size))
    return pl.pallas_call(
        functools.partial(dft_kernel, devices),
        grid=(shots // step,),
        in_specs=[
            pl.BlockSpec((1, channels, NT), lambda g, n=n: (g * step + n, 0, 0))
            for n in range(step)
        ]
        + [pl.BlockSpec(table.shape, lambda g: (0, 0, 0))],
        out_specs=pl.BlockSpec(memory_space=pltpu.VMEM),
        out_shape=jax.ShapeDtypeStruct((rows, LANES), jnp.float32),
        compiler_params=pltpu.CompilerParams(vmem_limit_bytes=40 * 2**20),
        cost_estimate=pl.CostEstimate(
            flops=3 * table.size * shots * channels,
            bytes_accessed=4 * (traces.size + rows * LANES),
            transcendentals=0,
        ),
    )(*[traces] * step, table)


def weights_kernel(w_ref, hi_ref, lo_ref):
    channels = w_ref.shape[2]
    for j in range(w_ref.shape[0]):
        for line in range(L):
            at = (pl.ds(j * channels, channels), pl.ds(line * P_SIZE, P_SIZE))
            hi_ref[at], lo_ref[at] = split(w_ref[j, line])


def split_weights(weights):
    freq_size, _, channels, _ = weights.shape
    out = jax.ShapeDtypeStruct((freq_size * channels, L * P_SIZE), jnp.bfloat16)
    return pl.pallas_call(
        weights_kernel,
        out_shape=(out, out),
        compiler_params=pltpu.CompilerParams(vmem_limit_bytes=48 * 2**20),
        cost_estimate=pl.CostEstimate(
            flops=10**11, bytes_accessed=8 * weights.size, transcendentals=0
        ),
    )(weights)


def panel_kernel(freq_size, count, *refs):
    rec_refs = refs[:count]
    (hi_ref, lo_ref, line_ref, src_ref, panel_ref, out_ref, a_hi, a_lo) = refs[count : count + 8]
    gathers = refs[count + 8 :]
    step = pl.program_id(0)
    steps = pl.num_programs(0)
    channels = hi_ref.shape[0] // freq_size
    tiles = rec_refs[0].shape[0] // (freq_size * ROWS)
    slots = tiles * LANES // channels

    low = lax.broadcasted_iota(jnp.int32, (ROWS, 2 * channels), 1) < channels
    for r, rec_ref in enumerate(rec_refs):
        for t in range(tiles):
            firsts, seconds = [], []
            for pair in range(freq_size // 2):
                a = rec_ref[pl.ds((2 * pair * tiles + t) * ROWS, ROWS), :]
                b = rec_ref[pl.ds(((2 * pair + 1) * tiles + t) * ROWS, ROWS), :]
                firsts.append(jnp.where(low, a, pltpu.roll(b, channels, 1)))
                seconds.append(jnp.where(low, pltpu.roll(a, channels, 1), b))
            both = jnp.concatenate(
                [jnp.concatenate(firsts, axis=1), jnp.concatenate(seconds, axis=1)], axis=0
            )
            at = pl.ds((r * slots + 2 * t) * ROWS, 2 * ROWS)
            a_hi[at, :], a_lo[at, :] = split(both)
    lines = dot3((a_hi[...], a_lo[...]), (hi_ref[...], lo_ref[...]))
    rows = count * slots * ROWS
    chosen = jnp.where(line_ref[...] == 0, lines[:, :P_SIZE], lines[:, P_SIZE:])
    for h, tile in enumerate(gathers):
        tile[pl.ds(pl.multiple_of(step * rows, rows), rows), :] = chosen[
            :, h * LANES : (h + 1) * LANES
        ]

    @pl.when(step == steps - 1)
    def _():
        shots = src_ref.shape[1]
        own = shots // out_ref.shape[0]
        source = split(src_ref[...])
        first = panel_ref[...] == 0
        for n in range(BINS):
            parts, panels = [], []
            for part in range(2):
                at = pl.ds(2 * n + part, shots, stride=2 * BINS)
                rows = jnp.concatenate([tile[at, :] for tile in gathers], axis=1)
                parts.append(split(rows))
                panels.append(dot3(source, parts[part]))
            chosen = None
            for k in range(K):
                at = slice(k * P_SIZE, (k + 1) * P_SIZE)
                real, imag = split(panels[0][at]), split(panels[1][at])
                out_real = dot3(parts[0], real) - dot3(parts[1], imag)
                out_imag = dot3(parts[0], imag) + dot3(parts[1], real)
                if k == 0:
                    chosen = (out_real, out_imag)
                else:
                    chosen = (
                        jnp.where(first, chosen[0], out_real),
                        jnp.where(first, chosen[1], out_imag),
                    )
            for part in range(2):
                for r in range(out_ref.shape[0]):
                    out_ref[r, n, part] = chosen[part][r * own : (r + 1) * own]


def panel_products(received, weights, lines, sources, panel_rows, freq_size, radon_size):
    depth, columns = weights[0].shape
    grid = 4
    count = radon_size // grid
    shots = sources.shape[1]
    rows = shots // grid * 2 * BINS
    out = (radon_size, BINS, 2, shots // radon_size, P_SIZE)
    return pl.pallas_call(
        functools.partial(panel_kernel, freq_size, count),
        grid=(grid,),
        in_specs=[
            pl.BlockSpec((received.shape[0] // radon_size, LANES), lambda r, n=n: (count * r + n, 0))
            for n in range(count)
        ]
        + [
            pl.BlockSpec((depth, columns), lambda r: (0, 0)),
            pl.BlockSpec((depth, columns), lambda r: (0, 0)),
            pl.BlockSpec((rows, 1), lambda r: (r, 0)),
            pl.BlockSpec(sources.shape, lambda r: (0, 0)),
            pl.BlockSpec((shots, 1), lambda r: (0, 0)),
        ],
        out_specs=pl.BlockSpec(out, lambda r: (0, 0, 0, 0, 0)),
        out_shape=jax.ShapeDtypeStruct(out, jnp.float32),
        scratch_shapes=[pltpu.VMEM((rows, depth), jnp.bfloat16)] * 2
        + [pltpu.VMEM((grid * rows, LANES), jnp.float32)] * (P_SIZE // LANES),
        compiler_params=pltpu.CompilerParams(vmem_limit_bytes=48 * 2**20),
        cost_estimate=pl.CostEstimate(
            flops=6 * grid * rows * depth * columns,
            bytes_accessed=4 * received.size,
            transcendentals=0,
        ),
    )(*[received] * count, *weights, lines, sources, panel_rows)


def shards(shot_traces, radon_weights, source_weights, line_index, panel_index):
    shot_rows = shot_traces.shape[0]
    freq_size = lax.axis_size("freq")
    radon_size = lax.axis_size("radon")

    weights = lax.all_gather(radon_weights, "freq", axis=0)
    weights = split_weights(weights)
    messages = dft(shot_traces, radon_size, freq_size)
    received = lax.all_to_all(messages, ("radon", "freq"), 0, 0, tiled=True)

    lines = jnp.repeat(line_index, 2 * BINS)[:, None]
    onehot = panel_index[None, :] == jnp.arange(K, dtype=jnp.int32)[:, None]
    sources = jnp.where(onehot[:, None, :], source_weights.T[None], 0.0).reshape(K * P_SIZE, -1)

    products = panel_products(
        received, weights, lines, sources, panel_index[:, None], freq_size, radon_size
    )
    result = lax.all_to_all(products, "radon", 0, 0, tiled=True)
    return result.reshape(BINS * radon_size, 2, shot_rows, P_SIZE)


def solution(mesh):
    placed = (P("radon", "freq", None), P(None, "freq", None), P(), P(), P())
    return jax.shard_map(
        shards,
        mesh=mesh,
        in_specs=placed,
        out_specs=P("freq", None, "radon", None),
        check_vma=False,
    )
```

```python
import functools

import jax
import jax.numpy as jnp
import ml_dtypes
import numpy as np
from jax import lax
from jax.experimental import pallas as pl
from jax.experimental.pallas import tpu as pltpu
from jax.sharding import PartitionSpec as P

NT = 1024
NF = 256
P_SIZE = 256
L = 2
K = 2
HALF = NT // 2
LANES = 128
BINS = 2
ROWS = 8
SPREAD = ROWS // 2


def split(x):
    hi = x.astype(jnp.bfloat16)
    lo = (x - hi.astype(jnp.float32)).astype(jnp.bfloat16)
    return hi, lo


def dot3(a, b):
    dot = functools.partial(jnp.dot, preferred_element_type=jnp.float32)
    return dot(a[0], b[0]) + (dot(a[0], b[1]) + dot(a[1], b[0]))


def dft_tables(radon_size, freq_size):
    band = NF // freq_size
    device = np.arange(radon_size * freq_size)
    rows = []
    for parity in range(BINS):
        bins = band * (device % freq_size) + BINS * (device // freq_size) + parity
        phase = (bins[:, None] * np.arange(HALF)[None, :] % NT) * (2.0 * np.pi / NT)
        rows += [np.cos(phase), -np.sin(phase)]
    table = (np.concatenate(rows) * NT ** (-0.5)).astype(np.float32)
    hi = table.astype(ml_dtypes.bfloat16)
    lo = (table - hi.astype(np.float32)).astype(ml_dtypes.bfloat16)
    return np.concatenate([hi, lo, hi], axis=1)


def dft_kernel(*refs):
    x_refs, (table_ref, out_ref), folded = refs[:2], refs[2:4], refs[4:]
    devices = out_ref.shape[0]
    groups, channels, _ = x_refs[0].shape
    message = BINS * ROWS
    flat_ref = out_ref.reshape(devices * message, LANES)
    for half in range(2):
        for parity in range(BINS):
            rows_ref = folded[half * BINS + parity]
            for n in range(2):
                for i in range(2):
                    shot = x_refs[i][half * 2 + n]
                    head, tail = shot[:, :HALF], shot[:, HALF:]
                    hi, lo = split(head - tail if parity else head + tail)
                    at = pl.ds((n * 2 + i) * channels, channels)
                    rows_ref[at, :HALF] = hi
                    rows_ref[at, HALF : 2 * HALF] = hi
                    rows_ref[at, 2 * HALF :] = lo
            at = slice(2 * parity * devices, 2 * (parity + 1) * devices)
            spectrum = lax.dot_general(
                table_ref[at],
                rows_ref[...],
                (((1,), (1,)), ((), ())),
                preferred_element_type=jnp.float32,
            )
            for n in range(2):
                for part in range(2):
                    row = parity * ROWS + 2 * (half * 2 + n) + part
                    flat_ref[pl.ds(row, devices, stride=message), :] = spectrum[
                        part * devices : (part + 1) * devices, n * LANES : (n + 1) * LANES
                    ]


def dft(traces, radon_size, freq_size):
    shots, channels, _ = traces.shape
    devices = radon_size * freq_size
    step = LANES // channels * SPREAD
    out = (devices, BINS, shots // step * ROWS, LANES)
    table = jnp.asarray(dft_tables(radon_size, freq_size))
    return pl.pallas_call(
        dft_kernel,
        grid=(shots // step,),
        in_specs=[
            pl.BlockSpec((step // 2, channels, NT), lambda g, n=n: (2 * g + n, 0, 0))
            for n in range(2)
        ]
        + [pl.BlockSpec(table.shape, lambda g: (0, 0))],
        out_specs=pl.BlockSpec((devices, BINS, ROWS, LANES), lambda g: (0, 0, g, 0)),
        out_shape=jax.ShapeDtypeStruct(out, jnp.float32),
        scratch_shapes=[pltpu.VMEM((4 * channels, 3 * HALF), jnp.bfloat16)] * (2 * BINS),
        compiler_params=pltpu.CompilerParams(vmem_limit_bytes=48 * 2**20),
        cost_estimate=pl.CostEstimate(
            flops=2 * table.size * shots * channels,
            bytes_accessed=6 * traces.size,
            transcendentals=0,
        ),
    )(traces, traces, table)


def weights_kernel(w_ref, out_ref):
    channels = w_ref.shape[2]
    for j in range(w_ref.shape[0]):
        for line in range(L):
            at = (pl.ds(j * channels, channels), pl.ds(line * P_SIZE, P_SIZE))
            hi, lo = split(w_ref[j, line])
            out_ref[0, at[0], at[1]] = hi
            out_ref[1, at[0], at[1]] = lo


def split_weights(weights):
    freq_size, _, channels, _ = weights.shape
    return pl.pallas_call(
        weights_kernel,
        out_shape=jax.ShapeDtypeStruct(
            (2, freq_size * channels, L * P_SIZE), jnp.bfloat16
        ),
        compiler_params=pltpu.CompilerParams(vmem_limit_bytes=32 * 2**20),
        cost_estimate=pl.CostEstimate(
            flops=10**11, bytes_accessed=8 * weights.size, transcendentals=0
        ),
    )(weights)


def panel_kernel(count, *refs):
    rec_refs, refs = refs[:count], refs[count:]
    (w_ref, line_ref, src_ref, panel_ref, out_ref, a_hi, a_lo), gathers = refs[:7], refs[7:]
    step = pl.program_id(0)
    steps = pl.num_programs(0)
    freq_size, bins, height, _ = rec_refs[0].shape
    channels = w_ref.shape[1] // freq_size
    tiles = height // ROWS

    low = lax.broadcasted_iota(jnp.int32, (ROWS, LANES), 1) < channels
    for parity in range(bins):
        for r, rec_ref in enumerate(rec_refs):
            for t in range(tiles):
                firsts, seconds = [], []
                for j in range(0, freq_size, 2):
                    a = rec_ref[j, parity, pl.ds(t * ROWS, ROWS), :]
                    b = rec_ref[j + 1, parity, pl.ds(t * ROWS, ROWS), :]
                    firsts.append(jnp.where(low, a, pltpu.roll(b, channels, 1)))
                    seconds.append(jnp.where(low, pltpu.roll(a, channels, 1), b))
                both = jnp.concatenate(
                    [jnp.concatenate(firsts, axis=1), jnp.concatenate(seconds, axis=1)], axis=0
                )
                at = pl.ds(((parity * count + r) * tiles + t) * 2 * ROWS, 2 * ROWS)
                a_hi[at, :], a_lo[at, :] = split(both)
    lines = dot3((a_hi[...], a_lo[...]), (w_ref[0], w_ref[1]))
    rows = a_hi.shape[0] // bins
    first_line = line_ref[...] == 0
    for parity in range(bins):
        own = lines[parity * rows : (parity + 1) * rows]
        chosen = jnp.where(first_line, own[:, :P_SIZE], own[:, P_SIZE:])
        for h in range(P_SIZE // LANES):
            gathers[parity * (P_SIZE // LANES) + h][
                pl.ds(pl.multiple_of(step * rows, rows), rows), :
            ] = chosen[:, h * LANES : (h + 1) * LANES]

    @pl.when(step == steps - 1)
    def _():
        shots = src_ref.shape[1]
        own = shots // out_ref.shape[0]
        source = split(src_ref[...])
        first = panel_ref[...] == 0
        for parity in range(bins):
            left, panels = ([], []), []
            for part in range(2):
                at = pl.ds(part, shots, stride=2)
                both = jnp.concatenate(
                    [
                        gathers[parity * (P_SIZE // LANES) + h][at, :]
                        for h in range(P_SIZE // LANES)
                    ],
                    axis=1,
                )
                panels.append(split(dot3(source, split(both))))
                for k in range(K):
                    hi, lo = split(jnp.where(first == (k == 0), both, 0.0))
                    left[0].append(hi)
                    left[1].append(lo)
            left = [jnp.concatenate(pieces, axis=1) for pieces in left]
            real, imag = panels
            rights = (
                [jnp.concatenate([real[n], -imag[n]], axis=0) for n in range(2)],
                [jnp.concatenate([imag[n], real[n]], axis=0) for n in range(2)],
            )
            for part in range(2):
                product = dot3(left, rights[part])
                for r in range(out_ref.shape[0]):
                    out_ref[r, parity, part] = product[r * own : (r + 1) * own]


def panel_products(received, weights, lines, sources, panel_rows, radon_size):
    _, depth, columns = weights.shape
    freq_size = received.shape[0] // radon_size
    grid = 4
    count = radon_size // grid
    shots = sources.shape[1]
    rows = shots // grid * 2
    out = (radon_size, BINS, 2, shots // radon_size, P_SIZE)
    return pl.pallas_call(
        functools.partial(panel_kernel, count),
        grid=(grid,),
        in_specs=[
            pl.BlockSpec(
                (freq_size,) + received.shape[1:], lambda r, n=n: (count * r + n, 0, 0, 0)
            )
            for n in range(count)
        ]
        + [
            pl.BlockSpec(weights.shape, lambda r: (0, 0, 0)),
            pl.BlockSpec((rows, 1), lambda r: (r, 0)),
            pl.BlockSpec(sources.shape, lambda r: (0, 0)),
            pl.BlockSpec((shots, 1), lambda r: (0, 0)),
        ],
        out_specs=pl.BlockSpec(out, lambda r: (0, 0, 0, 0, 0)),
        out_shape=jax.ShapeDtypeStruct(out, jnp.float32),
        scratch_shapes=[pltpu.VMEM((BINS * rows, depth), jnp.bfloat16)] * 2
        + [pltpu.VMEM((grid * rows, LANES), jnp.float32)] * (BINS * P_SIZE // LANES),
        compiler_params=pltpu.CompilerParams(vmem_limit_bytes=48 * 2**20),
        cost_estimate=pl.CostEstimate(
            flops=6 * grid * BINS * rows * depth * columns,
            bytes_accessed=4 * received.size,
            transcendentals=0,
        ),
    )(*[received] * count, weights, lines, sources, panel_rows)


def shards(shot_traces, radon_weights, source_weights, line_index, panel_index):
    shot_rows = shot_traces.shape[0]
    freq_size = lax.axis_size("freq")
    radon_size = lax.axis_size("radon")

    weights = split_weights(lax.all_gather(radon_weights, "freq", axis=0))
    messages = dft(shot_traces, radon_size, freq_size)
    received = lax.all_to_all(messages, ("radon", "freq"), 0, 0, tiled=True)

    lines = jnp.repeat(line_index, 2)[:, None]
    onehot = panel_index[None, :] == jnp.arange(K, dtype=jnp.int32)[:, None]
    sources = jnp.where(onehot[:, None, :], source_weights.T[None], 0.0).reshape(K * P_SIZE, -1)

    products = panel_products(
        received, weights, lines, sources, panel_index[:, None], radon_size
    )
    result = lax.all_to_all(products, "radon", 0, 0, tiled=True)
    return result.reshape(radon_size * BINS, 2, shot_rows, P_SIZE)


def solution(mesh):
    placed = (P("radon", "freq", None), P(None, "freq", None), P(), P(), P())
    return jax.shard_map(
        shards,
        mesh=mesh,
        in_specs=placed,
        out_specs=P("freq", None, "radon", None),
        check_vma=False,
    )
```

```python
import functools

import jax
import jax.numpy as jnp
import ml_dtypes
import numpy as np
from jax import lax
from jax.experimental import pallas as pl
from jax.experimental.pallas import tpu as pltpu
from jax.sharding import PartitionSpec as P

NT = 1024
NF = 256
P_SIZE = 256
L = 2
K = 2
HALF = NT // 2
LANES = 128
BINS = 2
ROWS = 8
SPREAD = ROWS // 2


def split(x):
    hi = x.astype(jnp.bfloat16)
    lo = (x - hi.astype(jnp.float32)).astype(jnp.bfloat16)
    return hi, lo


def dot3(a, b):
    dot = functools.partial(jnp.dot, preferred_element_type=jnp.float32)
    return dot(a[0], b[0]) + (dot(a[0], b[1]) + dot(a[1], b[0]))


def dft_tables(radon_size, freq_size):
    band = NF // freq_size
    device = np.arange(radon_size * freq_size)
    rows = []
    for parity in range(BINS):
        bins = band * (device % freq_size) + BINS * (device // freq_size) + parity
        phase = (bins[:, None] * np.arange(HALF)[None, :] % NT) * (2.0 * np.pi / NT)
        rows += [np.cos(phase), -np.sin(phase)]
    table = (np.concatenate(rows) * NT ** (-0.5)).astype(np.float32)
    hi = table.astype(ml_dtypes.bfloat16)
    lo = (table - hi.astype(np.float32)).astype(ml_dtypes.bfloat16)
    return np.concatenate([hi, lo, hi], axis=1)


def dft_kernel(x_hbm, table_hbm, out_hbm, x_buf, table, out_buf, *refs):
    folded, (x_sems, table_sem, out_sems) = refs[:-3], refs[-3:]
    steps, devices = out_buf.shape[:2]
    pieces, shots, channels, _ = x_buf.shape
    message = BINS * ROWS

    table_copy = pltpu.make_async_copy(table_hbm, table, table_sem)
    table_copy.start()

    def x_copy(n):
        return pltpu.make_async_copy(
            x_hbm.at[pl.ds(n * shots, shots)], x_buf.at[n], x_sems.at[n]
        )

    for n in range(pieces):
        x_copy(n).start()
    table_copy.wait()

    def out_copy(g):
        return pltpu.make_async_copy(
            out_buf.at[g], out_hbm.at[:, :, pl.ds(g * ROWS, ROWS), :], out_sems.at[g]
        )

    def body(g, carry):
        x_copy(2 * g).wait()
        x_copy(2 * g + 1).wait()
        flat_ref = out_buf.at[g].reshape(devices * message, LANES)
        for half in range(2):
            for parity in range(BINS):
                rows_ref = folded[half * BINS + parity]
                for n in range(2):
                    for i in range(2):
                        shot = x_buf[2 * g + i, half * 2 + n]
                        head, tail = shot[:, :HALF], shot[:, HALF:]
                        hi, lo = split(head - tail if parity else head + tail)
                        at = pl.ds((n * 2 + i) * channels, channels)
                        rows_ref[at, :HALF] = hi
                        rows_ref[at, HALF : 2 * HALF] = hi
                        rows_ref[at, 2 * HALF :] = lo
                at = slice(2 * parity * devices, 2 * (parity + 1) * devices)
                spectrum = lax.dot_general(
                    table[at],
                    rows_ref[...],
                    (((1,), (1,)), ((), ())),
                    preferred_element_type=jnp.float32,
                )
                for n in range(2):
                    for part in range(2):
                        row = parity * ROWS + 2 * (half * 2 + n) + part
                        flat_ref[pl.ds(row, devices, stride=message), :] = spectrum[
                            part * devices : (part + 1) * devices, n * LANES : (n + 1) * LANES
                        ]
        out_copy(g).start()
        return carry

    lax.fori_loop(0, steps, body, 0)
    for g in range(steps):
        out_copy(g).wait()


def dft(traces, radon_size, freq_size):
    shots, channels, _ = traces.shape
    devices = radon_size * freq_size
    step = LANES // channels * SPREAD
    steps = shots // step
    table = jnp.asarray(dft_tables(radon_size, freq_size))
    any_space = pl.BlockSpec(memory_space=pl.ANY)
    return pl.pallas_call(
        dft_kernel,
        in_specs=[any_space, any_space],
        out_specs=any_space,
        out_shape=jax.ShapeDtypeStruct((devices, BINS, steps * ROWS, LANES), jnp.float32),
        scratch_shapes=[
            pltpu.VMEM((2 * steps, step // 2, channels, NT), jnp.float32),
            pltpu.VMEM(table.shape, table.dtype),
            pltpu.VMEM((steps, devices, BINS, ROWS, LANES), jnp.float32),
        ]
        + [pltpu.VMEM((4 * channels, 3 * HALF), jnp.bfloat16)] * (2 * BINS)
        + [
            pltpu.SemaphoreType.DMA((2 * steps,)),
            pltpu.SemaphoreType.DMA,
            pltpu.SemaphoreType.DMA((steps,)),
        ],
        compiler_params=pltpu.CompilerParams(vmem_limit_bytes=60 * 2**20),
        cost_estimate=pl.CostEstimate(
            flops=2 * table.size * shots * channels,
            bytes_accessed=6 * traces.size,
            transcendentals=0,
        ),
    )(traces, table)


def weights_kernel(w_ref, out_ref):
    channels = w_ref.shape[2]
    for j in range(w_ref.shape[0]):
        for line in range(L):
            at = (pl.ds(j * channels, channels), pl.ds(line * P_SIZE, P_SIZE))
            hi, lo = split(w_ref[j, line])
            out_ref[0, at[0], at[1]] = hi
            out_ref[1, at[0], at[1]] = lo


def split_weights(weights):
    freq_size, _, channels, _ = weights.shape
    return pl.pallas_call(
        weights_kernel,
        out_shape=jax.ShapeDtypeStruct(
            (2, freq_size * channels, L * P_SIZE), jnp.bfloat16
        ),
        compiler_params=pltpu.CompilerParams(vmem_limit_bytes=32 * 2**20),
        cost_estimate=pl.CostEstimate(
            flops=10**11, bytes_accessed=8 * weights.size, transcendentals=0
        ),
    )(weights)


def panel_kernel(count, *refs):
    rec_refs, refs = refs[:count], refs[count:]
    (w_ref, line_ref, src_ref, panel_ref, out_ref, a_hi, a_lo), gathers = refs[:7], refs[7:]
    step = pl.program_id(0)
    steps = pl.num_programs(0)
    freq_size, bins, height, _ = rec_refs[0].shape
    channels = w_ref.shape[1] // freq_size
    tiles = height // ROWS

    low = lax.broadcasted_iota(jnp.int32, (ROWS, LANES), 1) < channels
    for parity in range(bins):
        for r, rec_ref in enumerate(rec_refs):
            for t in range(tiles):
                firsts, seconds = [], []
                for j in range(0, freq_size, 2):
                    a = rec_ref[j, parity, pl.ds(t * ROWS, ROWS), :]
                    b = rec_ref[j + 1, parity, pl.ds(t * ROWS, ROWS), :]
                    firsts.append(jnp.where(low, a, pltpu.roll(b, channels, 1)))
                    seconds.append(jnp.where(low, pltpu.roll(a, channels, 1), b))
                both = jnp.concatenate(
                    [jnp.concatenate(firsts, axis=1), jnp.concatenate(seconds, axis=1)], axis=0
                )
                at = pl.ds(((parity * count + r) * tiles + t) * 2 * ROWS, 2 * ROWS)
                a_hi[at, :], a_lo[at, :] = split(both)
    lines = dot3((a_hi[...], a_lo[...]), (w_ref[0], w_ref[1]))
    rows = a_hi.shape[0] // bins
    first_line = line_ref[...] == 0
    for parity in range(bins):
        own = lines[parity * rows : (parity + 1) * rows]
        chosen = jnp.where(first_line, own[:, :P_SIZE], own[:, P_SIZE:])
        for h in range(P_SIZE // LANES):
            gathers[parity * (P_SIZE // LANES) + h][
                pl.ds(pl.multiple_of(step * rows, rows), rows), :
            ] = chosen[:, h * LANES : (h + 1) * LANES]

    @pl.when(step == steps - 1)
    def _():
        shots = src_ref.shape[1]
        own = shots // out_ref.shape[0]
        source = split(src_ref[...])
        first = panel_ref[...] == 0
        for parity in range(bins):
            left, panels = ([], []), []
            for part in range(2):
                at = pl.ds(part, shots, stride=2)
                both = jnp.concatenate(
                    [
                        gathers[parity * (P_SIZE // LANES) + h][at, :]
                        for h in range(P_SIZE // LANES)
                    ],
                    axis=1,
                )
                panels.append(split(dot3(source, split(both))))
                for k in range(K):
                    hi, lo = split(jnp.where(first == (k == 0), both, 0.0))
                    left[0].append(hi)
                    left[1].append(lo)
            left = [jnp.concatenate(pieces, axis=1) for pieces in left]
            real, imag = panels
            rights = (
                [jnp.concatenate([real[n], -imag[n]], axis=0) for n in range(2)],
                [jnp.concatenate([imag[n], real[n]], axis=0) for n in range(2)],
            )
            for part in range(2):
                product = dot3(left, rights[part])
                for r in range(out_ref.shape[0]):
                    out_ref[r, parity, part] = product[r * own : (r + 1) * own]


def panel_products(received, weights, lines, sources, panel_rows, radon_size):
    _, depth, columns = weights.shape
    freq_size = received.shape[0] // radon_size
    grid = 2
    count = radon_size // grid
    shots = sources.shape[1]
    rows = shots // grid * 2
    out = (radon_size, BINS, 2, shots // radon_size, P_SIZE)
    return pl.pallas_call(
        functools.partial(panel_kernel, count),
        grid=(grid,),
        in_specs=[
            pl.BlockSpec(
                (freq_size,) + received.shape[1:], lambda r, n=n: (count * r + n, 0, 0, 0)
            )
            for n in range(count)
        ]
        + [
            pl.BlockSpec(weights.shape, lambda r: (0, 0, 0)),
            pl.BlockSpec((rows, 1), lambda r: (r, 0)),
            pl.BlockSpec(sources.shape, lambda r: (0, 0)),
            pl.BlockSpec((shots, 1), lambda r: (0, 0)),
        ],
        out_specs=pl.BlockSpec(out, lambda r: (0, 0, 0, 0, 0)),
        out_shape=jax.ShapeDtypeStruct(out, jnp.float32),
        scratch_shapes=[pltpu.VMEM((BINS * rows, depth), jnp.bfloat16)] * 2
        + [pltpu.VMEM((grid * rows, LANES), jnp.float32)] * (BINS * P_SIZE // LANES),
        compiler_params=pltpu.CompilerParams(vmem_limit_bytes=48 * 2**20),
        cost_estimate=pl.CostEstimate(
            flops=6 * grid * BINS * rows * depth * columns,
            bytes_accessed=4 * received.size,
            transcendentals=0,
        ),
    )(*[received] * count, weights, lines, sources, panel_rows)


def shards(shot_traces, radon_weights, source_weights, line_index, panel_index):
    shot_rows = shot_traces.shape[0]
    freq_size = lax.axis_size("freq")
    radon_size = lax.axis_size("radon")

    weights = split_weights(lax.all_gather(radon_weights, "freq", axis=0))
    messages = dft(shot_traces, radon_size, freq_size)
    received = lax.all_to_all(messages, ("radon", "freq"), 0, 0, tiled=True)

    lines = jnp.repeat(line_index, 2)[:, None]
    onehot = panel_index[None, :] == jnp.arange(K, dtype=jnp.int32)[:, None]
    sources = jnp.where(onehot[:, None, :], source_weights.T[None], 0.0).reshape(K * P_SIZE, -1)

    products = panel_products(
        received, weights, lines, sources, panel_index[:, None], radon_size
    )
    result = lax.all_to_all(products, "radon", 0, 0, tiled=True)
    return result.reshape(radon_size * BINS, 2, shot_rows, P_SIZE)


def solution(mesh):
    placed = (P("radon", "freq", None), P(None, "freq", None), P(), P(), P())
    return jax.shard_map(
        shards,
        mesh=mesh,
        in_specs=placed,
        out_specs=P("freq", None, "radon", None),
        check_vma=False,
    )
```

```python
import functools

import jax
import jax.numpy as jnp
import ml_dtypes
import numpy as np
from jax import lax
from jax.experimental import pallas as pl
from jax.experimental.pallas import tpu as pltpu
from jax.sharding import PartitionSpec as P

NT = 1024
NF = 256
P_SIZE = 256
L = 2
K = 2
HALF = NT // 2
LANES = 128
BINS = 2
ROWS = 8
SPREAD = ROWS // 2


def split(x):
    hi = x.astype(jnp.bfloat16)
    lo = (x - hi.astype(jnp.float32)).astype(jnp.bfloat16)
    return hi, lo


def dot3(a, b):
    dot = functools.partial(jnp.dot, preferred_element_type=jnp.float32)
    return dot(a[0], b[0]) + (dot(a[0], b[1]) + dot(a[1], b[0]))


def dft_tables(radon_size, freq_size):
    band = NF // freq_size
    device = np.arange(radon_size * freq_size)
    rows = []
    for parity in range(BINS):
        bins = band * (device % freq_size) + BINS * (device // freq_size) + parity
        phase = (bins[:, None] * np.arange(HALF)[None, :] % NT) * (2.0 * np.pi / NT)
        rows.append(np.stack([np.cos(phase), -np.sin(phase)], axis=1).reshape(-1, HALF))
    table = (np.concatenate(rows) * NT ** (-0.5)).astype(np.float32)
    hi = table.astype(ml_dtypes.bfloat16)
    lo = (table - hi.astype(np.float32)).astype(ml_dtypes.bfloat16)
    return np.concatenate([hi, lo, hi], axis=1)


def trade(pieces, block):
    first, second = pieces
    row = lax.broadcasted_iota(jnp.int32, first.shape, 1)
    stay = lax.rem(lax.div(row, block), 2) == 0
    return (
        jnp.where(stay, first, pltpu.roll(second, block, 1)),
        jnp.where(stay, pltpu.roll(first, ROWS - block, 1), second),
    )


def dft_kernel(x_hbm, table_hbm, out_hbm, x_buf, table, out_buf, *refs):
    folded, (x_sems, table_sem, out_sems) = refs[:-3], refs[-3:]
    steps = out_buf.shape[0]
    pieces, shots, channels, _ = x_buf.shape
    count = table.shape[0] // BINS

    table_copy = pltpu.make_async_copy(table_hbm, table, table_sem)
    table_copy.start()

    def x_copy(n):
        return pltpu.make_async_copy(
            x_hbm.at[pl.ds(n * shots, shots)], x_buf.at[n], x_sems.at[n]
        )

    for n in range(pieces):
        x_copy(n).start()
    table_copy.wait()

    def out_copy(g):
        return pltpu.make_async_copy(
            out_buf.at[g], out_hbm.at[:, :, :, pl.ds(g * ROWS, ROWS), :], out_sems.at[g]
        )

    def body(g, carry):
        x_copy(2 * g).wait()
        x_copy(2 * g + 1).wait()
        for sh in range(SPREAD):
            for i in range(2):
                shot = x_buf[2 * g + i, sh]
                head, tail = shot[:, :HALF], shot[:, HALF:]
                at = pl.ds((sh * 2 + i) * channels, channels)
                for rows_ref, rows in zip(folded, (head + tail, head - tail)):
                    hi, lo = split(rows)
                    rows_ref[at, :HALF] = hi
                    rows_ref[at, HALF : 2 * HALF] = hi
                    rows_ref[at, 2 * HALF :] = lo
        for parity in range(BINS):
            shot_rows = []
            for half in range(2):
                spectrum = lax.dot_general(
                    table[parity * count : (parity + 1) * count],
                    folded[parity][half * 2 * LANES : (half + 1) * 2 * LANES],
                    (((1,), (1,)), ((), ())),
                    preferred_element_type=jnp.float32,
                )
                for n in range(2):
                    shot_rows.append(
                        spectrum[:, n * LANES : (n + 1) * LANES].reshape(-1, ROWS, LANES)
                    )
            a0, a2 = trade((shot_rows[0], shot_rows[2]), 4)
            a1, a3 = trade((shot_rows[1], shot_rows[3]), 4)
            devices = trade((a0, a1), 2) + trade((a2, a3), 2)
            for n, rows in enumerate(devices):
                out_buf[g, :, n, parity] = rows
        out_copy(g).start()
        return carry

    lax.fori_loop(0, steps, body, 0)
    for g in range(steps):
        out_copy(g).wait()


def dft(traces, radon_size, freq_size):
    shots, channels, _ = traces.shape
    devices = radon_size * freq_size
    step = LANES // channels * SPREAD
    steps = shots // step
    table = jnp.asarray(dft_tables(radon_size, freq_size))
    any_space = pl.BlockSpec(memory_space=pl.ANY)
    groups = (devices // SPREAD, SPREAD, BINS)
    out = pl.pallas_call(
        dft_kernel,
        in_specs=[any_space, any_space],
        out_specs=any_space,
        out_shape=jax.ShapeDtypeStruct(groups + (steps * ROWS, LANES), jnp.float32),
        scratch_shapes=[
            pltpu.VMEM((2 * steps, step // 2, channels, NT), jnp.float32),
            pltpu.VMEM(table.shape, table.dtype),
            pltpu.VMEM((steps,) + groups + (ROWS, LANES), jnp.float32),
        ]
        + [pltpu.VMEM((step * channels, 3 * HALF), jnp.bfloat16)] * BINS
        + [
            pltpu.SemaphoreType.DMA((2 * steps,)),
            pltpu.SemaphoreType.DMA,
            pltpu.SemaphoreType.DMA((steps,)),
        ],
        compiler_params=pltpu.CompilerParams(vmem_limit_bytes=60 * 2**20),
        cost_estimate=pl.CostEstimate(
            flops=2 * table.size * shots * channels,
            bytes_accessed=6 * traces.size,
            transcendentals=0,
        ),
    )(traces, table)
    return out.reshape(devices, BINS, steps * ROWS, LANES)


def weights_kernel(w_ref, out_ref):
    channels = w_ref.shape[2]
    for j in range(w_ref.shape[0]):
        for line in range(L):
            at = (pl.ds(j * channels, channels), pl.ds(line * P_SIZE, P_SIZE))
            hi, lo = split(w_ref[j, line])
            out_ref[0, at[0], at[1]] = hi
            out_ref[1, at[0], at[1]] = lo


def split_weights(weights):
    freq_size, _, channels, _ = weights.shape
    return pl.pallas_call(
        weights_kernel,
        out_shape=jax.ShapeDtypeStruct(
            (2, freq_size * channels, L * P_SIZE), jnp.bfloat16
        ),
        compiler_params=pltpu.CompilerParams(vmem_limit_bytes=32 * 2**20),
        cost_estimate=pl.CostEstimate(
            flops=10**11, bytes_accessed=8 * weights.size, transcendentals=0
        ),
    )(weights)


def panel_kernel(count, *refs):
    rec_refs, refs = refs[:count], refs[count:]
    (w_ref, line_ref, src_ref, panel_ref, out_ref, a_hi, a_lo), gathers = refs[:7], refs[7:]
    step = pl.program_id(0)
    steps = pl.num_programs(0)
    freq_size, bins, height, _ = rec_refs[0].shape
    channels = w_ref.shape[1] // freq_size
    tiles = height // ROWS

    low = lax.broadcasted_iota(jnp.int32, (ROWS, LANES), 1) < channels
    for parity in range(bins):
        for r, rec_ref in enumerate(rec_refs):
            for t in range(tiles):
                firsts, seconds = [], []
                for j in range(0, freq_size, 2):
                    a = rec_ref[j, parity, pl.ds(t * ROWS, ROWS), :]
                    b = rec_ref[j + 1, parity, pl.ds(t * ROWS, ROWS), :]
                    firsts.append(jnp.where(low, a, pltpu.roll(b, channels, 1)))
                    seconds.append(jnp.where(low, pltpu.roll(a, channels, 1), b))
                both = jnp.concatenate(
                    [jnp.concatenate(firsts, axis=1), jnp.concatenate(seconds, axis=1)], axis=0
                )
                at = pl.ds(((parity * count + r) * tiles + t) * 2 * ROWS, 2 * ROWS)
                a_hi[at, :], a_lo[at, :] = split(both)
    lines = dot3((a_hi[...], a_lo[...]), (w_ref[0], w_ref[1]))
    rows = a_hi.shape[0] // bins
    first_line = line_ref[...] == 0
    for parity in range(bins):
        own = lines[parity * rows : (parity + 1) * rows]
        chosen = jnp.where(first_line, own[:, :P_SIZE], own[:, P_SIZE:])
        for h in range(P_SIZE // LANES):
            gathers[parity * (P_SIZE // LANES) + h][
                pl.ds(pl.multiple_of(step * rows, rows), rows), :
            ] = chosen[:, h * LANES : (h + 1) * LANES]

    @pl.when(step == steps - 1)
    def _():
        shots = src_ref.shape[1]
        own = shots // out_ref.shape[0]
        source = split(src_ref[...])
        first = panel_ref[...] == 0
        for parity in range(bins):
            left, panels = ([], []), []
            for part in range(2):
                at = pl.ds(part, shots, stride=2)
                both = jnp.concatenate(
                    [
                        gathers[parity * (P_SIZE // LANES) + h][at, :]
                        for h in range(P_SIZE // LANES)
                    ],
                    axis=1,
                )
                panels.append(split(dot3(source, split(both))))
                for k in range(K):
                    hi, lo = split(jnp.where(first == (k == 0), both, 0.0))
                    left[0].append(hi)
                    left[1].append(lo)
            left = [jnp.concatenate(pieces, axis=1) for pieces in left]
            real, imag = panels
            rights = (
                [jnp.concatenate([real[n], -imag[n]], axis=0) for n in range(2)],
                [jnp.concatenate([imag[n], real[n]], axis=0) for n in range(2)],
            )
            for part in range(2):
                product = dot3(left, rights[part])
                for r in range(out_ref.shape[0]):
                    out_ref[r, parity, part] = product[r * own : (r + 1) * own]


def panel_products(received, weights, lines, sources, panel_rows, radon_size):
    _, depth, columns = weights.shape
    freq_size = received.shape[0] // radon_size
    grid = 2
    count = radon_size // grid
    shots = sources.shape[1]
    rows = shots // grid * 2
    out = (radon_size, BINS, 2, shots // radon_size, P_SIZE)
    return pl.pallas_call(
        functools.partial(panel_kernel, count),
        grid=(grid,),
        in_specs=[
            pl.BlockSpec(
                (freq_size,) + received.shape[1:], lambda r, n=n: (count * r + n, 0, 0, 0)
            )
            for n in range(count)
        ]
        + [
            pl.BlockSpec(weights.shape, lambda r: (0, 0, 0)),
            pl.BlockSpec((rows, 1), lambda r: (r, 0)),
            pl.BlockSpec(sources.shape, lambda r: (0, 0)),
            pl.BlockSpec((shots, 1), lambda r: (0, 0)),
        ],
        out_specs=pl.BlockSpec(out, lambda r: (0, 0, 0, 0, 0)),
        out_shape=jax.ShapeDtypeStruct(out, jnp.float32),
        scratch_shapes=[pltpu.VMEM((BINS * rows, depth), jnp.bfloat16)] * 2
        + [pltpu.VMEM((grid * rows, LANES), jnp.float32)] * (BINS * P_SIZE // LANES),
        compiler_params=pltpu.CompilerParams(vmem_limit_bytes=48 * 2**20),
        cost_estimate=pl.CostEstimate(
            flops=6 * grid * BINS * rows * depth * columns,
            bytes_accessed=4 * received.size,
            transcendentals=0,
        ),
    )(*[received] * count, weights, lines, sources, panel_rows)


def shards(shot_traces, radon_weights, source_weights, line_index, panel_index):
    shot_rows = shot_traces.shape[0]
    freq_size = lax.axis_size("freq")
    radon_size = lax.axis_size("radon")

    weights = split_weights(lax.all_gather(radon_weights, "freq", axis=0))
    messages = dft(shot_traces, radon_size, freq_size)
    received = lax.all_to_all(messages, ("radon", "freq"), 0, 0, tiled=True)

    lines = jnp.repeat(line_index, 2)[:, None]
    onehot = panel_index[None, :] == jnp.arange(K, dtype=jnp.int32)[:, None]
    sources = jnp.where(onehot[:, None, :], source_weights.T[None], 0.0).reshape(K * P_SIZE, -1)

    products = panel_products(
        received, weights, lines, sources, panel_index[:, None], radon_size
    )
    result = lax.all_to_all(products, "radon", 0, 0, tiled=True)
    return result.reshape(radon_size * BINS, 2, shot_rows, P_SIZE)


def solution(mesh):
    placed = (P("radon", "freq", None), P(None, "freq", None), P(), P(), P())
    return jax.shard_map(
        shards,
        mesh=mesh,
        in_specs=placed,
        out_specs=P("freq", None, "radon", None),
        check_vma=False,
    )
```

```python
import functools

import jax
import jax.numpy as jnp
import ml_dtypes
import numpy as np
from jax import lax
from jax.experimental import pallas as pl
from jax.experimental.pallas import tpu as pltpu
from jax.sharding import PartitionSpec as P

NT = 1024
NF = 256
P_SIZE = 256
L = 2
K = 2
HALF = NT // 2
LANES = 128
BINS = 2
ROWS = 8
SPREAD = ROWS // 2


def split(x):
    hi = x.astype(jnp.bfloat16)
    lo = (x - hi.astype(jnp.float32)).astype(jnp.bfloat16)
    return hi, lo


def dot3(a, b):
    dot = functools.partial(jnp.dot, preferred_element_type=jnp.float32)
    return dot(a[0], b[0]) + (dot(a[0], b[1]) + dot(a[1], b[0]))


def dft_tables(radon_size, freq_size):
    band = NF // freq_size
    device = np.arange(radon_size * freq_size)
    rows = []
    for parity in range(BINS):
        bins = band * (device % freq_size) + BINS * (device // freq_size) + parity
        phase = (bins[:, None] * np.arange(HALF)[None, :] % NT) * (2.0 * np.pi / NT)
        rows.append(np.stack([np.cos(phase), -np.sin(phase)], axis=1).reshape(-1, HALF))
    table = (np.concatenate(rows) * NT ** (-0.5)).astype(np.float32)
    hi = table.astype(ml_dtypes.bfloat16)
    lo = (table - hi.astype(np.float32)).astype(ml_dtypes.bfloat16)
    return np.concatenate([hi, lo], axis=1)


def trade(pieces, block):
    first, second = pieces
    row = lax.broadcasted_iota(jnp.int32, first.shape, 1)
    stay = lax.rem(lax.div(row, block), 2) == 0
    return (
        jnp.where(stay, first, pltpu.roll(second, block, 1)),
        jnp.where(stay, pltpu.roll(first, ROWS - block, 1), second),
    )


def dft_kernel(line_ref, x_hbm, table_hbm, out_hbm, x_buf, table, out_buf, *refs):
    folded, (order, x_sems, table_sem, out_sems) = refs[:-4], refs[-4:]
    steps = out_buf.shape[0]
    shots, channels, _ = x_buf.shape
    step = shots // steps
    count = table.shape[0] // BINS

    table_copy = pltpu.make_async_copy(table_hbm, table.at[:, : 2 * HALF], table_sem)
    table_copy.start()

    offset = lax.axis_index("radon") * shots

    def place(shot, counts):
        line = line_ref[offset + shot]
        order[jnp.where(line == 0, counts[0], counts[1])] = shot
        return (counts[0] + (1 - line), counts[1] + line)

    lax.fori_loop(0, shots, place, (jnp.int32(0), jnp.int32(shots // L)))

    def x_copy(n):
        return pltpu.make_async_copy(x_hbm.at[order[n]], x_buf.at[n], x_sems.at[n])

    def out_copy(g):
        return pltpu.make_async_copy(
            out_buf.at[g], out_hbm.at[:, :, :, pl.ds(g * ROWS, ROWS), :], out_sems.at[g]
        )

    for n in range(2 * step):
        x_copy(n).start()
    table_copy.wait()
    table[:, 2 * HALF :] = table[:, :HALF]

    def body(g, carry):
        for n in range(step):
            x_copy(g * step + n).wait()

        @pl.when(g + 2 < steps)
        def _():
            for n in range(step):
                x_copy((g + 2) * step + n).start()

        for sh in range(SPREAD):
            for i in range(2):
                shot = x_buf[g * step + SPREAD * i + sh]
                head, tail = shot[:, :HALF], shot[:, HALF:]
                at = pl.ds((sh * 2 + i) * channels, channels)
                for rows_ref, rows in zip(folded, (head + tail, head - tail)):
                    hi, lo = split(rows)
                    rows_ref[at, :HALF] = hi
                    rows_ref[at, HALF : 2 * HALF] = hi
                    rows_ref[at, 2 * HALF :] = lo
        for parity in range(BINS):
            shot_rows = []
            for half in range(2):
                spectrum = lax.dot_general(
                    table[parity * count : (parity + 1) * count],
                    folded[parity][half * 2 * LANES : (half + 1) * 2 * LANES],
                    (((1,), (1,)), ((), ())),
                    preferred_element_type=jnp.float32,
                )
                for n in range(2):
                    shot_rows.append(
                        spectrum[:, n * LANES : (n + 1) * LANES].reshape(-1, ROWS, LANES)
                    )
            a0, a2 = trade((shot_rows[0], shot_rows[2]), 4)
            a1, a3 = trade((shot_rows[1], shot_rows[3]), 4)
            devices = trade((a0, a1), 2) + trade((a2, a3), 2)
            for n, rows in enumerate(devices):
                out_buf[g, :, n, parity] = rows
        out_copy(g).start()
        return carry

    lax.fori_loop(0, steps, body, 0)
    for g in range(steps):
        out_copy(g).wait()


def dft(line_index, traces, radon_size, freq_size):
    shots, channels, _ = traces.shape
    devices = radon_size * freq_size
    step = LANES // channels * SPREAD
    steps = shots // step
    table = jnp.asarray(dft_tables(radon_size, freq_size))
    any_space = pl.BlockSpec(memory_space=pl.ANY)
    groups = (devices // SPREAD, SPREAD, BINS)
    out = pl.pallas_call(
        dft_kernel,
        in_specs=[pl.BlockSpec(memory_space=pltpu.SMEM), any_space, any_space],
        out_specs=any_space,
        out_shape=jax.ShapeDtypeStruct(groups + (steps * ROWS, LANES), jnp.float32),
        scratch_shapes=[
            pltpu.VMEM(traces.shape, jnp.float32),
            pltpu.VMEM((table.shape[0], 3 * HALF), table.dtype),
            pltpu.VMEM((steps,) + groups + (ROWS, LANES), jnp.float32),
        ]
        + [pltpu.VMEM((step * channels, 3 * HALF), jnp.bfloat16)] * BINS
        + [
            pltpu.SMEM((shots,), jnp.int32),
            pltpu.SemaphoreType.DMA((shots,)),
            pltpu.SemaphoreType.DMA,
            pltpu.SemaphoreType.DMA((steps,)),
        ],
        compiler_params=pltpu.CompilerParams(vmem_limit_bytes=60 * 2**20),
        cost_estimate=pl.CostEstimate(
            flops=3 * table.size * shots * channels,
            bytes_accessed=6 * traces.size,
            transcendentals=0,
        ),
    )(line_index, traces, table)
    return out.reshape(devices, BINS, steps * ROWS, LANES)


def weights_kernel(w_ref, out_ref):
    channels = w_ref.shape[2]
    for j in range(w_ref.shape[0]):
        for line in range(L):
            at = (pl.ds(j * channels, channels), pl.ds(line * P_SIZE, P_SIZE))
            hi, lo = split(w_ref[j, line])
            out_ref[0, at[0], at[1]] = hi
            out_ref[1, at[0], at[1]] = lo


def split_weights(weights):
    freq_size, _, channels, _ = weights.shape
    return pl.pallas_call(
        weights_kernel,
        out_shape=jax.ShapeDtypeStruct(
            (2, freq_size * channels, L * P_SIZE), jnp.bfloat16
        ),
        compiler_params=pltpu.CompilerParams(vmem_limit_bytes=32 * 2**20),
        cost_estimate=pl.CostEstimate(
            flops=10**11, bytes_accessed=8 * weights.size, transcendentals=0
        ),
    )(weights)


def panel_kernel(count, *refs):
    rec_refs, refs = refs[:count], refs[count:]
    (w_ref, src_ref, panel_ref, back_ref, out_ref), refs = refs[:5], refs[5:]
    a_refs, gathers = refs[: 2 * L], refs[2 * L :]
    step = pl.program_id(0)
    steps = pl.num_programs(0)
    freq_size, bins, height, _ = rec_refs[0].shape
    channels = w_ref.shape[1] // freq_size
    tiles = height // ROWS // L
    halves = P_SIZE // LANES

    low = lax.broadcasted_iota(jnp.int32, (ROWS, LANES), 1) < channels
    rows = tiles * 2 * ROWS
    for line in range(L):
        a_hi, a_lo = a_refs[2 * line : 2 * line + 2]
        for parity in range(bins):
            for r, rec_ref in enumerate(rec_refs):
                for t in range(tiles):
                    firsts, seconds = [], []
                    for j in range(0, freq_size, 2):
                        at = pl.ds((line * tiles + t) * ROWS, ROWS)
                        a = rec_ref[j, parity, at, :]
                        b = rec_ref[j + 1, parity, at, :]
                        firsts.append(jnp.where(low, a, pltpu.roll(b, channels, 1)))
                        seconds.append(jnp.where(low, pltpu.roll(a, channels, 1), b))
                    both = jnp.concatenate(
                        [jnp.concatenate(firsts, axis=1), jnp.concatenate(seconds, axis=1)],
                        axis=0,
                    )
                    at = pl.ds((parity * count + r) * rows + t * 2 * ROWS, 2 * ROWS)
                    a_hi[at, :], a_lo[at, :] = split(both)
        weights = w_ref[0, :, line * P_SIZE : (line + 1) * P_SIZE], w_ref[
            1, :, line * P_SIZE : (line + 1) * P_SIZE
        ]
        found = dot3((a_hi[...], a_lo[...]), weights)
        for parity in range(bins):
            for r in range(count):
                start = pl.multiple_of(((step * count + r) * L + line) * rows, rows)
                own = found[(parity * count + r) * rows : (parity * count + r + 1) * rows]
                for h in range(halves):
                    gathers[parity * halves + h][pl.ds(start, rows), :] = own[
                        :, h * LANES : (h + 1) * LANES
                    ]

    @pl.when(step == steps - 1)
    def _():
        shots = src_ref.shape[1]
        own = shots // out_ref.shape[0]
        source = split(src_ref[...])
        first = panel_ref[...] == 0
        blocks, block, _ = back_ref.shape
        for parity in range(bins):
            left, panels = ([], []), []
            for part in range(2):
                at = pl.ds(part, shots, stride=2)
                sorted_rows = jnp.concatenate(
                    split(
                        jnp.concatenate(
                            [gathers[parity * halves + h][at, :] for h in range(halves)], axis=1
                        )
                    ),
                    axis=1,
                )
                natural = jnp.concatenate(
                    [
                        jnp.dot(
                            back_ref[n],
                            sorted_rows[n * block : (n + 1) * block],
                            preferred_element_type=jnp.float32,
                        )
                        for n in range(blocks)
                    ],
                    axis=0,
                )
                pieces = natural[:, :P_SIZE], natural[:, P_SIZE:]
                panels.append(
                    split(dot3(source, [piece.astype(jnp.bfloat16) for piece in pieces]))
                )
                for k in range(K):
                    for kept, piece in zip(left, pieces):
                        chosen = jnp.where(first == (k == 0), piece, 0.0)
                        kept.append(chosen.astype(jnp.bfloat16))
            left = [jnp.concatenate(kept, axis=1) for kept in left]
            real, imag = panels
            rights = (
                [jnp.concatenate([real[n], -imag[n]], axis=0) for n in range(2)],
                [jnp.concatenate([imag[n], real[n]], axis=0) for n in range(2)],
            )
            for part in range(2):
                product = dot3(left, rights[part])
                for r in range(out_ref.shape[0]):
                    out_ref[r, parity, part] = product[r * own : (r + 1) * own]


def panel_products(received, weights, sources, panel_rows, back, radon_size):
    _, depth, columns = weights.shape
    freq_size = received.shape[0] // radon_size
    grid = 2
    count = radon_size // grid
    shots = sources.shape[1]
    rows = shots // grid * 2
    out = (radon_size, BINS, 2, shots // radon_size, P_SIZE)
    return pl.pallas_call(
        functools.partial(panel_kernel, count),
        grid=(grid,),
        in_specs=[
            pl.BlockSpec(
                (freq_size,) + received.shape[1:], lambda r, n=n: (count * r + n, 0, 0, 0)
            )
            for n in range(count)
        ]
        + [
            pl.BlockSpec(weights.shape, lambda r: (0, 0, 0)),
            pl.BlockSpec(sources.shape, lambda r: (0, 0)),
            pl.BlockSpec((shots, 1), lambda r: (0, 0)),
            pl.BlockSpec(back.shape, lambda r: (0, 0, 0)),
        ],
        out_specs=pl.BlockSpec(out, lambda r: (0, 0, 0, 0, 0)),
        out_shape=jax.ShapeDtypeStruct(out, jnp.float32),
        scratch_shapes=[pltpu.VMEM((BINS * rows // L, depth), jnp.bfloat16)] * (2 * L)
        + [pltpu.VMEM((grid * rows, LANES), jnp.float32)] * (BINS * P_SIZE // LANES),
        compiler_params=pltpu.CompilerParams(vmem_limit_bytes=48 * 2**20),
        cost_estimate=pl.CostEstimate(
            flops=6 * grid * BINS * rows * depth * P_SIZE,
            bytes_accessed=4 * received.size,
            transcendentals=0,
        ),
    )(*[received] * count, weights, sources, panel_rows, back)


def back_to_order(line_index, radon_size, blocks):
    lines = line_index.reshape(radon_size, -1)
    own = lines.shape[1]
    ranks = [jnp.cumsum((lines == line).astype(jnp.int32), axis=1) - 1 for line in range(L)]
    place = jnp.where(lines == 0, ranks[0], ranks[1] + own // L)
    place = place + own * (jnp.arange(radon_size, dtype=jnp.int32) % (radon_size // blocks))[:, None]
    place = place.reshape(blocks, -1)
    spots = jnp.arange(place.shape[1], dtype=jnp.int32)
    return (place[:, :, None] == spots[None, None, :]).astype(jnp.bfloat16)


def shards(shot_traces, radon_weights, source_weights, line_index, panel_index):
    shot_rows = shot_traces.shape[0]
    freq_size = lax.axis_size("freq")
    radon_size = lax.axis_size("radon")

    weights = split_weights(lax.all_gather(radon_weights, "freq", axis=0))
    messages = dft(line_index, shot_traces, radon_size, freq_size)
    received = lax.all_to_all(messages, ("radon", "freq"), 0, 0, tiled=True)

    onehot = panel_index[None, :] == jnp.arange(K, dtype=jnp.int32)[:, None]
    sources = jnp.where(onehot[:, None, :], source_weights.T[None], 0.0).reshape(K * P_SIZE, -1)

    back = back_to_order(line_index, radon_size, 2)
    products = panel_products(
        received, weights, sources, panel_index[:, None], back, radon_size
    )
    result = lax.all_to_all(products, "radon", 0, 0, tiled=True)
    return result.reshape(radon_size * BINS, 2, shot_rows, P_SIZE)


def solution(mesh):
    placed = (P("radon", "freq", None), P(None, "freq", None), P(), P(), P())
    return jax.shard_map(
        shards,
        mesh=mesh,
        in_specs=placed,
        out_specs=P("freq", None, "radon", None),
        check_vma=False,
    )
```

```python
import functools

import jax
import jax.numpy as jnp
import ml_dtypes
import numpy as np
from jax import lax
from jax.experimental import pallas as pl
from jax.experimental.pallas import tpu as pltpu
from jax.sharding import PartitionSpec as P

NT = 1024
NF = 256
P_SIZE = 256
L = 2
K = 2
HALF = NT // 2
LANES = 128
BINS = 2
ROWS = 8
SPREAD = ROWS // 2
AHEAD = 3


def split(x):
    hi = x.astype(jnp.bfloat16)
    lo = (x - hi.astype(jnp.float32)).astype(jnp.bfloat16)
    return hi, lo


def dot3(a, b):
    dot = functools.partial(jnp.dot, preferred_element_type=jnp.float32)
    return dot(a[0], b[0]) + (dot(a[0], b[1]) + dot(a[1], b[0]))


def dft_tables(radon_size, freq_size):
    band = NF // freq_size
    device = np.arange(radon_size * freq_size)
    rows = []
    for parity in range(BINS):
        bins = band * (device % freq_size) + BINS * (device // freq_size) + parity
        phase = (bins[:, None] * np.arange(HALF)[None, :] % NT) * (2.0 * np.pi / NT)
        rows.append(np.stack([np.cos(phase), -np.sin(phase)], axis=1).reshape(-1, HALF))
    table = (np.concatenate(rows) * NT ** (-0.5)).astype(np.float32)
    hi = table.astype(ml_dtypes.bfloat16)
    lo = (table - hi.astype(np.float32)).astype(ml_dtypes.bfloat16)
    return np.concatenate([hi, lo], axis=1)


def trade(pieces, block):
    first, second = pieces
    row = lax.broadcasted_iota(jnp.int32, first.shape, 1)
    stay = lax.rem(lax.div(row, block), 2) == 0
    return (
        jnp.where(stay, first, pltpu.roll(second, block, 1)),
        jnp.where(stay, pltpu.roll(first, ROWS - block, 1), second),
    )


def dft_kernel(line_ref, x_hbm, table_hbm, out_hbm, x_buf, table, out_buf, *refs):
    folded, (order, x_sems, table_sem, out_sems) = refs[:-4], refs[-4:]
    steps = out_buf.shape[0]
    shots, channels, _ = x_buf.shape
    step = shots // steps
    count = table.shape[0] // BINS

    table_copy = pltpu.make_async_copy(table_hbm, table.at[:, : 2 * HALF], table_sem)
    table_copy.start()

    offset = lax.axis_index("radon") * shots

    def place(shot, counts):
        line = line_ref[offset + shot]
        order[jnp.where(line == 0, counts[0], counts[1])] = shot
        return (counts[0] + (1 - line), counts[1] + line)

    lax.fori_loop(0, shots, place, (jnp.int32(0), jnp.int32(shots // L)))

    def x_copy(n):
        return pltpu.make_async_copy(x_hbm.at[order[n]], x_buf.at[n], x_sems.at[n])

    def out_copy(g):
        return pltpu.make_async_copy(
            out_buf.at[g], out_hbm.at[:, :, :, pl.ds(g * ROWS, ROWS), :], out_sems.at[g]
        )

    for n in range(AHEAD * step):
        x_copy(n).start()
    table_copy.wait()
    table[:, 2 * HALF :] = table[:, :HALF]

    def body(g, carry):
        for n in range(step):
            x_copy(g * step + n).wait()

        @pl.when(g + AHEAD < steps)
        def _():
            for n in range(step):
                x_copy((g + AHEAD) * step + n).start()

        for sh in range(SPREAD):
            for i in range(2):
                shot = x_buf[g * step + SPREAD * i + sh]
                head, tail = shot[:, :HALF], shot[:, HALF:]
                at = pl.ds((sh * 2 + i) * channels, channels)
                for rows_ref, rows in zip(folded, (head + tail, head - tail)):
                    hi, lo = split(rows)
                    rows_ref[at, :HALF] = hi
                    rows_ref[at, HALF : 2 * HALF] = hi
                    rows_ref[at, 2 * HALF :] = lo
        for parity in range(BINS):
            shot_rows = []
            for half in range(2):
                spectrum = lax.dot_general(
                    table[parity * count : (parity + 1) * count],
                    folded[parity][half * 2 * LANES : (half + 1) * 2 * LANES],
                    (((1,), (1,)), ((), ())),
                    preferred_element_type=jnp.float32,
                )
                for n in range(2):
                    shot_rows.append(
                        spectrum[:, n * LANES : (n + 1) * LANES].reshape(-1, ROWS, LANES)
                    )
            a0, a2 = trade((shot_rows[0], shot_rows[2]), 4)
            a1, a3 = trade((shot_rows[1], shot_rows[3]), 4)
            devices = trade((a0, a1), 2) + trade((a2, a3), 2)
            for n, rows in enumerate(devices):
                out_buf[g, :, n, parity] = rows
        out_copy(g).start()
        return carry

    lax.fori_loop(0, steps, body, 0)
    for g in range(steps):
        out_copy(g).wait()


def dft(line_index, traces, radon_size, freq_size):
    shots, channels, _ = traces.shape
    devices = radon_size * freq_size
    step = LANES // channels * SPREAD
    steps = shots // step
    table = jnp.asarray(dft_tables(radon_size, freq_size))
    any_space = pl.BlockSpec(memory_space=pl.ANY)
    groups = (devices // SPREAD, SPREAD, BINS)
    out = pl.pallas_call(
        dft_kernel,
        in_specs=[pl.BlockSpec(memory_space=pltpu.SMEM), any_space, any_space],
        out_specs=any_space,
        out_shape=jax.ShapeDtypeStruct(groups + (steps * ROWS, LANES), jnp.float32),
        scratch_shapes=[
            pltpu.VMEM(traces.shape, jnp.float32),
            pltpu.VMEM((table.shape[0], 3 * HALF), table.dtype),
            pltpu.VMEM((steps,) + groups + (ROWS, LANES), jnp.float32),
        ]
        + [pltpu.VMEM((step * channels, 3 * HALF), jnp.bfloat16)] * BINS
        + [
            pltpu.SMEM((shots,), jnp.int32),
            pltpu.SemaphoreType.DMA((shots,)),
            pltpu.SemaphoreType.DMA,
            pltpu.SemaphoreType.DMA((steps,)),
        ],
        compiler_params=pltpu.CompilerParams(vmem_limit_bytes=60 * 2**20),
        cost_estimate=pl.CostEstimate(
            flops=3 * table.size * shots * channels,
            bytes_accessed=6 * traces.size,
            transcendentals=0,
        ),
    )(line_index, traces, table)
    return out.reshape(devices, BINS, steps * ROWS, LANES)


def weights_kernel(own_ref, other_ref, out_ref):
    chips, _, channels, _ = own_ref.shape
    even = lax.rem(lax.axis_index("freq"), 2) == 0
    for chip in range(chips):
        for line in range(L):
            own, other = own_ref[chip, line], other_ref[chip, line]
            pair = jnp.where(even, own, other), jnp.where(even, other, own)
            for core in range(2):
                hi, lo = split(pair[core])
                at = (
                    pl.ds((2 * chip + core) * channels, channels),
                    pl.ds(line * P_SIZE, P_SIZE),
                )
                out_ref[0, at[0], at[1]] = hi
                out_ref[1, at[0], at[1]] = lo


def all_weights(weights, freq_size):
    groups = [list(range(core, freq_size, 2)) for core in range(2)]
    own = lax.all_gather(weights, "freq", axis=0, axis_index_groups=groups)
    other = lax.ppermute(own, "freq", [(j, j ^ 1) for j in range(freq_size)])
    chips, _, channels, _ = own.shape
    return pl.pallas_call(
        weights_kernel,
        out_shape=jax.ShapeDtypeStruct(
            (2, 2 * chips * channels, L * P_SIZE), jnp.bfloat16
        ),
        compiler_params=pltpu.CompilerParams(vmem_limit_bytes=32 * 2**20),
        cost_estimate=pl.CostEstimate(
            flops=10**11, bytes_accessed=16 * own.size, transcendentals=0
        ),
    )(own, other)


def panel_kernel(count, *refs):
    rec_refs, refs = refs[:count], refs[count:]
    (w_ref, src_ref, panel_ref, back_ref, out_ref), refs = refs[:5], refs[5:]
    a_refs, gathers = refs[: 2 * L], refs[2 * L :]
    step = pl.program_id(0)
    steps = pl.num_programs(0)
    freq_size, bins, height, _ = rec_refs[0].shape
    channels = w_ref.shape[1] // freq_size
    tiles = height // ROWS // L
    halves = P_SIZE // LANES

    low = lax.broadcasted_iota(jnp.int32, (ROWS, LANES), 1) < channels
    rows = tiles * 2 * ROWS
    for line in range(L):
        a_hi, a_lo = a_refs[2 * line : 2 * line + 2]
        for parity in range(bins):
            for r, rec_ref in enumerate(rec_refs):
                for t in range(tiles):
                    firsts, seconds = [], []
                    for j in range(0, freq_size, 2):
                        at = pl.ds((line * tiles + t) * ROWS, ROWS)
                        a = rec_ref[j, parity, at, :]
                        b = rec_ref[j + 1, parity, at, :]
                        firsts.append(jnp.where(low, a, pltpu.roll(b, channels, 1)))
                        seconds.append(jnp.where(low, pltpu.roll(a, channels, 1), b))
                    both = jnp.concatenate(
                        [jnp.concatenate(firsts, axis=1), jnp.concatenate(seconds, axis=1)],
                        axis=0,
                    )
                    at = pl.ds((parity * count + r) * rows + t * 2 * ROWS, 2 * ROWS)
                    a_hi[at, :], a_lo[at, :] = split(both)
        weights = w_ref[0, :, line * P_SIZE : (line + 1) * P_SIZE], w_ref[
            1, :, line * P_SIZE : (line + 1) * P_SIZE
        ]
        found = dot3((a_hi[...], a_lo[...]), weights)
        for parity in range(bins):
            for r in range(count):
                start = pl.multiple_of(((step * count + r) * L + line) * rows, rows)
                own = found[(parity * count + r) * rows : (parity * count + r + 1) * rows]
                for h in range(halves):
                    gathers[parity * halves + h][pl.ds(start, rows), :] = own[
                        :, h * LANES : (h + 1) * LANES
                    ]

    @pl.when(step == steps - 1)
    def _():
        shots = src_ref.shape[1]
        own = shots // out_ref.shape[0]
        source = split(src_ref[...])
        first = panel_ref[...] == 0
        blocks, block, _ = back_ref.shape
        for parity in range(bins):
            left, panels = ([], []), []
            for part in range(2):
                at = pl.ds(part, shots, stride=2)
                sorted_rows = jnp.concatenate(
                    split(
                        jnp.concatenate(
                            [gathers[parity * halves + h][at, :] for h in range(halves)], axis=1
                        )
                    ),
                    axis=1,
                )
                natural = jnp.concatenate(
                    [
                        jnp.dot(
                            back_ref[n],
                            sorted_rows[n * block : (n + 1) * block],
                            preferred_element_type=jnp.float32,
                        )
                        for n in range(blocks)
                    ],
                    axis=0,
                )
                pieces = natural[:, :P_SIZE], natural[:, P_SIZE:]
                panels.append(
                    split(dot3(source, [piece.astype(jnp.bfloat16) for piece in pieces]))
                )
                for k in range(K):
                    for kept, piece in zip(left, pieces):
                        chosen = jnp.where(first == (k == 0), piece, 0.0)
                        kept.append(chosen.astype(jnp.bfloat16))
            left = [jnp.concatenate(kept, axis=1) for kept in left]
            real, imag = panels
            rights = (
                [jnp.concatenate([real[n], -imag[n]], axis=0) for n in range(2)],
                [jnp.concatenate([imag[n], real[n]], axis=0) for n in range(2)],
            )
            for part in range(2):
                product = dot3(left, rights[part])
                for r in range(out_ref.shape[0]):
                    out_ref[r, parity, part] = product[r * own : (r + 1) * own]


def panel_products(received, weights, sources, panel_rows, back, radon_size):
    _, depth, columns = weights.shape
    freq_size = received.shape[0] // radon_size
    grid = 2
    count = radon_size // grid
    shots = sources.shape[1]
    rows = shots // grid * 2
    out = (radon_size, BINS, 2, shots // radon_size, P_SIZE)
    return pl.pallas_call(
        functools.partial(panel_kernel, count),
        grid=(grid,),
        in_specs=[
            pl.BlockSpec(
                (freq_size,) + received.shape[1:], lambda r, n=n: (count * r + n, 0, 0, 0)
            )
            for n in range(count)
        ]
        + [
            pl.BlockSpec(weights.shape, lambda r: (0, 0, 0)),
            pl.BlockSpec(sources.shape, lambda r: (0, 0)),
            pl.BlockSpec((shots, 1), lambda r: (0, 0)),
            pl.BlockSpec(back.shape, lambda r: (0, 0, 0)),
        ],
        out_specs=pl.BlockSpec(out, lambda r: (0, 0, 0, 0, 0)),
        out_shape=jax.ShapeDtypeStruct(out, jnp.float32),
        scratch_shapes=[pltpu.VMEM((BINS * rows // L, depth), jnp.bfloat16)] * (2 * L)
        + [pltpu.VMEM((grid * rows, LANES), jnp.float32)] * (BINS * P_SIZE // LANES),
        compiler_params=pltpu.CompilerParams(vmem_limit_bytes=48 * 2**20),
        cost_estimate=pl.CostEstimate(
            flops=6 * grid * BINS * rows * depth * P_SIZE,
            bytes_accessed=4 * received.size,
            transcendentals=0,
        ),
    )(*[received] * count, weights, sources, panel_rows, back)


def back_to_order(line_index, radon_size, blocks):
    lines = line_index.reshape(radon_size, -1)
    own = lines.shape[1]
    ranks = [jnp.cumsum((lines == line).astype(jnp.int32), axis=1) - 1 for line in range(L)]
    place = jnp.where(lines == 0, ranks[0], ranks[1] + own // L)
    place = place + own * (jnp.arange(radon_size, dtype=jnp.int32) % (radon_size // blocks))[:, None]
    place = place.reshape(blocks, -1)
    spots = jnp.arange(place.shape[1], dtype=jnp.int32)
    return (place[:, :, None] == spots[None, None, :]).astype(jnp.bfloat16)


def shards(shot_traces, radon_weights, source_weights, line_index, panel_index):
    shot_rows = shot_traces.shape[0]
    freq_size = lax.axis_size("freq")
    radon_size = lax.axis_size("radon")

    weights = all_weights(radon_weights, freq_size)
    messages = dft(line_index, shot_traces, radon_size, freq_size)
    received = lax.all_to_all(messages, ("radon", "freq"), 0, 0, tiled=True)

    onehot = panel_index[None, :] == jnp.arange(K, dtype=jnp.int32)[:, None]
    sources = jnp.where(onehot[:, None, :], source_weights.T[None], 0.0).reshape(K * P_SIZE, -1)

    back = back_to_order(line_index, radon_size, 2)
    products = panel_products(
        received, weights, sources, panel_index[:, None], back, radon_size
    )
    result = lax.all_to_all(products, "radon", 0, 0, tiled=True)
    return result.reshape(radon_size * BINS, 2, shot_rows, P_SIZE)


def solution(mesh):
    placed = (P("radon", "freq", None), P(None, "freq", None), P(), P(), P())
    return jax.shard_map(
        shards,
        mesh=mesh,
        in_specs=placed,
        out_specs=P("freq", None, "radon", None),
        check_vma=False,
    )
```

```python
import functools

import jax
import jax.numpy as jnp
import ml_dtypes
import numpy as np
from jax import lax
from jax.experimental import pallas as pl
from jax.experimental.pallas import tpu as pltpu
from jax.sharding import PartitionSpec as P

NT = 1024
NF = 256
P_SIZE = 256
L = 2
K = 2
HALF = NT // 2
LANES = 128
BINS = 2
ROWS = 8
SPREAD = ROWS // 2
AHEAD = 3
GRID = 2


def split(x):
    hi = x.astype(jnp.bfloat16)
    lo = (x - hi.astype(jnp.float32)).astype(jnp.bfloat16)
    return hi, lo


def dot3(a, b):
    dot = functools.partial(jnp.dot, preferred_element_type=jnp.float32)
    return dot(a[0], b[0]) + (dot(a[0], b[1]) + dot(a[1], b[0]))


def exchange_order(radon_size, freq_size):
    mixed = np.random.RandomState(7).permutation(radon_size // GRID * freq_size)
    return mixed, np.concatenate([mixed + n * mixed.size for n in range(GRID)])


def dft_tables(radon_size, freq_size):
    band = NF // freq_size
    _, device = exchange_order(radon_size, freq_size)
    rows = []
    for parity in range(BINS):
        bins = band * (device % freq_size) + BINS * (device // freq_size) + parity
        phase = (bins[:, None] * np.arange(HALF)[None, :] % NT) * (2.0 * np.pi / NT)
        rows.append(np.stack([np.cos(phase), -np.sin(phase)], axis=1).reshape(-1, HALF))
    table = (np.concatenate(rows) * NT ** (-0.5)).astype(np.float32)
    hi = table.astype(ml_dtypes.bfloat16)
    lo = (table - hi.astype(np.float32)).astype(ml_dtypes.bfloat16)
    return np.concatenate([hi, lo], axis=1)


def trade(pieces, block):
    first, second = pieces
    row = lax.broadcasted_iota(jnp.int32, first.shape, 1)
    stay = lax.rem(lax.div(row, block), 2) == 0
    return (
        jnp.where(stay, first, pltpu.roll(second, block, 1)),
        jnp.where(stay, pltpu.roll(first, ROWS - block, 1), second),
    )


def dft_kernel(line_ref, x_hbm, table_hbm, out_hbm, x_buf, table, out_buf, *refs):
    folded, (order, x_sems, table_sem, out_sems) = refs[:-4], refs[-4:]
    steps = out_buf.shape[0]
    shots, channels, _ = x_buf.shape
    step = shots // steps
    count = table.shape[0] // BINS

    table_copy = pltpu.make_async_copy(table_hbm, table.at[:, : 2 * HALF], table_sem)
    table_copy.start()

    offset = lax.axis_index("radon") * shots

    def place(shot, counts):
        line = line_ref[offset + shot]
        order[jnp.where(line == 0, counts[0], counts[1])] = shot
        return (counts[0] + (1 - line), counts[1] + line)

    lax.fori_loop(0, shots, place, (jnp.int32(0), jnp.int32(shots // L)))

    def x_copy(n):
        return pltpu.make_async_copy(x_hbm.at[order[n]], x_buf.at[n], x_sems.at[n])

    def out_copy(g):
        return pltpu.make_async_copy(
            out_buf.at[g], out_hbm.at[:, :, :, pl.ds(g * ROWS, ROWS), :], out_sems.at[g]
        )

    for n in range(AHEAD * step):
        x_copy(n).start()
    table_copy.wait()
    table[:, 2 * HALF :] = table[:, :HALF]

    def body(g, carry):
        for n in range(step):
            x_copy(g * step + n).wait()

        @pl.when(g + AHEAD < steps)
        def _():
            for n in range(step):
                x_copy((g + AHEAD) * step + n).start()

        for sh in range(SPREAD):
            for i in range(2):
                shot = x_buf[g * step + SPREAD * i + sh]
                head, tail = shot[:, :HALF], shot[:, HALF:]
                at = pl.ds((sh * 2 + i) * channels, channels)
                for rows_ref, rows in zip(folded, (head + tail, head - tail)):
                    hi, lo = split(rows)
                    rows_ref[at, :HALF] = hi
                    rows_ref[at, HALF : 2 * HALF] = hi
                    rows_ref[at, 2 * HALF :] = lo
        for parity in range(BINS):
            shot_rows = []
            for half in range(2):
                spectrum = lax.dot_general(
                    table[parity * count : (parity + 1) * count],
                    folded[parity][half * 2 * LANES : (half + 1) * 2 * LANES],
                    (((1,), (1,)), ((), ())),
                    preferred_element_type=jnp.float32,
                )
                for n in range(2):
                    shot_rows.append(
                        spectrum[:, n * LANES : (n + 1) * LANES].reshape(-1, ROWS, LANES)
                    )
            a0, a2 = trade((shot_rows[0], shot_rows[2]), 4)
            a1, a3 = trade((shot_rows[1], shot_rows[3]), 4)
            devices = trade((a0, a1), 2) + trade((a2, a3), 2)
            for n, rows in enumerate(devices):
                out_buf[g, :, n, parity] = rows
        out_copy(g).start()
        return carry

    lax.fori_loop(0, steps, body, 0)
    for g in range(steps):
        out_copy(g).wait()


def dft(line_index, traces, radon_size, freq_size):
    shots, channels, _ = traces.shape
    devices = radon_size * freq_size
    step = LANES // channels * SPREAD
    steps = shots // step
    table = jnp.asarray(dft_tables(radon_size, freq_size))
    any_space = pl.BlockSpec(memory_space=pl.ANY)
    groups = (devices // SPREAD, SPREAD, BINS)
    out = pl.pallas_call(
        dft_kernel,
        in_specs=[pl.BlockSpec(memory_space=pltpu.SMEM), any_space, any_space],
        out_specs=any_space,
        out_shape=jax.ShapeDtypeStruct(groups + (steps * ROWS, LANES), jnp.float32),
        scratch_shapes=[
            pltpu.VMEM(traces.shape, jnp.float32),
            pltpu.VMEM((table.shape[0], 3 * HALF), table.dtype),
            pltpu.VMEM((steps,) + groups + (ROWS, LANES), jnp.float32),
        ]
        + [pltpu.VMEM((step * channels, 3 * HALF), jnp.bfloat16)] * BINS
        + [
            pltpu.SMEM((shots,), jnp.int32),
            pltpu.SemaphoreType.DMA((shots,)),
            pltpu.SemaphoreType.DMA,
            pltpu.SemaphoreType.DMA((steps,)),
        ],
        compiler_params=pltpu.CompilerParams(vmem_limit_bytes=60 * 2**20),
        cost_estimate=pl.CostEstimate(
            flops=3 * table.size * shots * channels,
            bytes_accessed=6 * traces.size,
            transcendentals=0,
        ),
    )(line_index, traces, table)
    return out.reshape(devices, BINS, steps * ROWS, LANES)


def weights_kernel(w_ref, out_ref):
    channels = w_ref.shape[2]
    for j in range(w_ref.shape[0]):
        for line in range(L):
            at = (pl.ds(j * channels, channels), pl.ds(line * P_SIZE, P_SIZE))
            hi, lo = split(w_ref[j, line])
            out_ref[0, at[0], at[1]] = hi
            out_ref[1, at[0], at[1]] = lo


def split_weights(weights):
    freq_size, _, channels, _ = weights.shape
    return pl.pallas_call(
        weights_kernel,
        out_shape=jax.ShapeDtypeStruct(
            (2, freq_size * channels, L * P_SIZE), jnp.bfloat16
        ),
        compiler_params=pltpu.CompilerParams(vmem_limit_bytes=32 * 2**20),
        cost_estimate=pl.CostEstimate(
            flops=10**11, bytes_accessed=8 * weights.size, transcendentals=0
        ),
    )(weights)


def panel_kernel(spots, freq_size, *refs):
    count = spots.size // freq_size
    rec_refs, refs = refs[:count], refs[count:]
    (w_ref, src_ref, panel_ref, back_ref, out_ref), refs = refs[:5], refs[5:]
    a_refs, gathers = refs[: 2 * L], refs[2 * L :]
    step = pl.program_id(0)
    steps = pl.num_programs(0)
    _, bins, height, _ = rec_refs[0].shape
    channels = w_ref.shape[1] // freq_size
    tiles = height // ROWS // L
    halves = P_SIZE // LANES

    low = lax.broadcasted_iota(jnp.int32, (ROWS, LANES), 1) < channels
    rows = tiles * 2 * ROWS
    for line in range(L):
        a_hi, a_lo = a_refs[2 * line : 2 * line + 2]
        for parity in range(bins):
            for r in range(count):
                for t in range(tiles):
                    firsts, seconds = [], []
                    for j in range(0, freq_size, 2):
                        at = pl.ds((line * tiles + t) * ROWS, ROWS)
                        a, b = (
                            rec_refs[spot // freq_size][spot % freq_size, parity, at, :]
                            for spot in spots[r * freq_size + j : r * freq_size + j + 2]
                        )
                        firsts.append(jnp.where(low, a, pltpu.roll(b, channels, 1)))
                        seconds.append(jnp.where(low, pltpu.roll(a, channels, 1), b))
                    both = jnp.concatenate(
                        [jnp.concatenate(firsts, axis=1), jnp.concatenate(seconds, axis=1)],
                        axis=0,
                    )
                    at = pl.ds((parity * count + r) * rows + t * 2 * ROWS, 2 * ROWS)
                    a_hi[at, :], a_lo[at, :] = split(both)
        weights = w_ref[0, :, line * P_SIZE : (line + 1) * P_SIZE], w_ref[
            1, :, line * P_SIZE : (line + 1) * P_SIZE
        ]
        found = dot3((a_hi[...], a_lo[...]), weights)
        for parity in range(bins):
            for r in range(count):
                start = pl.multiple_of(((step * count + r) * L + line) * rows, rows)
                own = found[(parity * count + r) * rows : (parity * count + r + 1) * rows]
                for h in range(halves):
                    gathers[parity * halves + h][pl.ds(start, rows), :] = own[
                        :, h * LANES : (h + 1) * LANES
                    ]

    @pl.when(step == steps - 1)
    def _():
        shots = src_ref.shape[1]
        own = shots // out_ref.shape[0]
        source = split(src_ref[...])
        first = panel_ref[...] == 0
        blocks, block, _ = back_ref.shape
        for parity in range(bins):
            left, panels = ([], []), []
            for part in range(2):
                at = pl.ds(part, shots, stride=2)
                sorted_rows = jnp.concatenate(
                    split(
                        jnp.concatenate(
                            [gathers[parity * halves + h][at, :] for h in range(halves)], axis=1
                        )
                    ),
                    axis=1,
                )
                natural = jnp.concatenate(
                    [
                        jnp.dot(
                            back_ref[n],
                            sorted_rows[n * block : (n + 1) * block],
                            preferred_element_type=jnp.float32,
                        )
                        for n in range(blocks)
                    ],
                    axis=0,
                )
                pieces = natural[:, :P_SIZE], natural[:, P_SIZE:]
                panels.append(
                    split(dot3(source, [piece.astype(jnp.bfloat16) for piece in pieces]))
                )
                for k in range(K):
                    for kept, piece in zip(left, pieces):
                        chosen = jnp.where(first == (k == 0), piece, 0.0)
                        kept.append(chosen.astype(jnp.bfloat16))
            left = [jnp.concatenate(kept, axis=1) for kept in left]
            real, imag = panels
            rights = (
                [jnp.concatenate([real[n], -imag[n]], axis=0) for n in range(2)],
                [jnp.concatenate([imag[n], real[n]], axis=0) for n in range(2)],
            )
            for part in range(2):
                product = dot3(left, rights[part])
                for r in range(out_ref.shape[0]):
                    out_ref[r, parity, part] = product[r * own : (r + 1) * own]


def panel_products(received, weights, sources, panel_rows, back, radon_size):
    _, depth, columns = weights.shape
    freq_size = received.shape[0] // radon_size
    grid = GRID
    count = radon_size // grid
    spots = np.argsort(exchange_order(radon_size, freq_size)[0])
    shots = sources.shape[1]
    rows = shots // grid * 2
    out = (radon_size, BINS, 2, shots // radon_size, P_SIZE)
    return pl.pallas_call(
        functools.partial(panel_kernel, spots, freq_size),
        grid=(grid,),
        in_specs=[
            pl.BlockSpec(
                (freq_size,) + received.shape[1:], lambda r, n=n: (count * r + n, 0, 0, 0)
            )
            for n in range(count)
        ]
        + [
            pl.BlockSpec(weights.shape, lambda r: (0, 0, 0)),
            pl.BlockSpec(sources.shape, lambda r: (0, 0)),
            pl.BlockSpec((shots, 1), lambda r: (0, 0)),
            pl.BlockSpec(back.shape, lambda r: (0, 0, 0)),
        ],
        out_specs=pl.BlockSpec(out, lambda r: (0, 0, 0, 0, 0)),
        out_shape=jax.ShapeDtypeStruct(out, jnp.float32),
        scratch_shapes=[pltpu.VMEM((BINS * rows // L, depth), jnp.bfloat16)] * (2 * L)
        + [pltpu.VMEM((grid * rows, LANES), jnp.float32)] * (BINS * P_SIZE // LANES),
        compiler_params=pltpu.CompilerParams(vmem_limit_bytes=48 * 2**20),
        cost_estimate=pl.CostEstimate(
            flops=6 * grid * BINS * rows * depth * P_SIZE,
            bytes_accessed=4 * received.size,
            transcendentals=0,
        ),
    )(*[received] * count, weights, sources, panel_rows, back)


def back_to_order(line_index, radon_size, blocks):
    lines = line_index.reshape(radon_size, -1)
    own = lines.shape[1]
    ranks = [jnp.cumsum((lines == line).astype(jnp.int32), axis=1) - 1 for line in range(L)]
    place = jnp.where(lines == 0, ranks[0], ranks[1] + own // L)
    place = place + own * (jnp.arange(radon_size, dtype=jnp.int32) % (radon_size // blocks))[:, None]
    place = place.reshape(blocks, -1)
    spots = jnp.arange(place.shape[1], dtype=jnp.int32)
    return (place[:, :, None] == spots[None, None, :]).astype(jnp.bfloat16)


def shards(shot_traces, radon_weights, source_weights, line_index, panel_index):
    shot_rows = shot_traces.shape[0]
    freq_size = lax.axis_size("freq")
    radon_size = lax.axis_size("radon")

    weights = split_weights(lax.all_gather(radon_weights, "freq", axis=0))
    messages = dft(line_index, shot_traces, radon_size, freq_size)
    _, order = exchange_order(radon_size, freq_size)
    received = lax.all_to_all(
        messages, ("radon", "freq"), 0, 0, axis_index_groups=[order.tolist()], tiled=True
    )

    onehot = panel_index[None, :] == jnp.arange(K, dtype=jnp.int32)[:, None]
    sources = jnp.where(onehot[:, None, :], source_weights.T[None], 0.0).reshape(K * P_SIZE, -1)

    back = back_to_order(line_index, radon_size, 2)
    products = panel_products(
        received, weights, sources, panel_index[:, None], back, radon_size
    )
    result = lax.all_to_all(products, "radon", 0, 0, tiled=True)
    return result.reshape(radon_size * BINS, 2, shot_rows, P_SIZE)


def solution(mesh):
    placed = (P("radon", "freq", None), P(None, "freq", None), P(), P(), P())
    return jax.shard_map(
        shards,
        mesh=mesh,
        in_specs=placed,
        out_specs=P("freq", None, "radon", None),
        check_vma=False,
    )
```

```python
import functools

import jax
import jax.numpy as jnp
import ml_dtypes
import numpy as np
from jax import lax
from jax.experimental import pallas as pl
from jax.experimental.pallas import tpu as pltpu
from jax.sharding import PartitionSpec as P

NT = 1024
NF = 256
P_SIZE = 256
L = 2
K = 2
HALF = NT // 2
LANES = 128
BINS = 2
ROWS = 8
SPREAD = ROWS // 2
AHEAD = 3
GRID = 2


def split(x):
    hi = x.astype(jnp.bfloat16)
    lo = (x - hi.astype(jnp.float32)).astype(jnp.bfloat16)
    return hi, lo


def dot3(a, b):
    dot = functools.partial(jnp.dot, preferred_element_type=jnp.float32)
    return dot(a[0], b[0]) + (dot(a[0], b[1]) + dot(a[1], b[0]))


def exchange_order(radon_size, freq_size):
    depth = radon_size // 2
    sources = [depth * y_lo + z for z in range(depth) for y_lo in range(2)]
    half = freq_size // 2
    devices = [
        (depth * y_lo + z) * freq_size + half * y_hi + n
        for z in range(depth)
        for y_hi in range(2)
        for y_lo in range(2)
        for n in range(half)
    ]
    count = radon_size // GRID
    spots = [devices.index(r * freq_size + j) for r in sources[:count] for j in range(freq_size)]
    return sources, spots, devices


def dft_tables(radon_size, freq_size):
    band = NF // freq_size
    device = np.array(exchange_order(radon_size, freq_size)[2])
    rows = []
    for parity in range(BINS):
        bins = band * (device % freq_size) + BINS * (device // freq_size) + parity
        phase = (bins[:, None] * np.arange(HALF)[None, :] % NT) * (2.0 * np.pi / NT)
        rows.append(np.stack([np.cos(phase), -np.sin(phase)], axis=1).reshape(-1, HALF))
    table = (np.concatenate(rows) * NT ** (-0.5)).astype(np.float32)
    hi = table.astype(ml_dtypes.bfloat16)
    lo = (table - hi.astype(np.float32)).astype(ml_dtypes.bfloat16)
    return np.concatenate([hi, lo], axis=1)


def trade(pieces, block):
    first, second = pieces
    row = lax.broadcasted_iota(jnp.int32, first.shape, 1)
    stay = lax.rem(lax.div(row, block), 2) == 0
    return (
        jnp.where(stay, first, pltpu.roll(second, block, 1)),
        jnp.where(stay, pltpu.roll(first, ROWS - block, 1), second),
    )


def dft_kernel(line_ref, x_hbm, table_hbm, out_hbm, x_buf, table, out_buf, *refs):
    folded, (order, x_sems, table_sem, out_sems) = refs[:-4], refs[-4:]
    steps = out_buf.shape[0]
    shots, channels, _ = x_buf.shape
    step = shots // steps
    count = table.shape[0] // BINS

    table_copy = pltpu.make_async_copy(table_hbm, table.at[:, : 2 * HALF], table_sem)
    table_copy.start()

    offset = lax.axis_index("radon") * shots

    def place(shot, counts):
        line = line_ref[offset + shot]
        order[jnp.where(line == 0, counts[0], counts[1])] = shot
        return (counts[0] + (1 - line), counts[1] + line)

    lax.fori_loop(0, shots, place, (jnp.int32(0), jnp.int32(shots // L)))

    def x_copy(n):
        return pltpu.make_async_copy(x_hbm.at[order[n]], x_buf.at[n], x_sems.at[n])

    def out_copy(g):
        return pltpu.make_async_copy(
            out_buf.at[g], out_hbm.at[:, :, :, pl.ds(g * ROWS, ROWS), :], out_sems.at[g]
        )

    for n in range(AHEAD * step):
        x_copy(n).start()
    table_copy.wait()
    table[:, 2 * HALF :] = table[:, :HALF]

    def body(g, carry):
        for n in range(step):
            x_copy(g * step + n).wait()

        @pl.when(g + AHEAD < steps)
        def _():
            for n in range(step):
                x_copy((g + AHEAD) * step + n).start()

        for sh in range(SPREAD):
            for i in range(2):
                shot = x_buf[g * step + SPREAD * i + sh]
                head, tail = shot[:, :HALF], shot[:, HALF:]
                at = pl.ds((sh * 2 + i) * channels, channels)
                for rows_ref, rows in zip(folded, (head + tail, head - tail)):
                    hi, lo = split(rows)
                    rows_ref[at, :HALF] = hi
                    rows_ref[at, HALF : 2 * HALF] = hi
                    rows_ref[at, 2 * HALF :] = lo
        for parity in range(BINS):
            shot_rows = []
            for half in range(2):
                spectrum = lax.dot_general(
                    table[parity * count : (parity + 1) * count],
                    folded[parity][half * 2 * LANES : (half + 1) * 2 * LANES],
                    (((1,), (1,)), ((), ())),
                    preferred_element_type=jnp.float32,
                )
                for n in range(2):
                    shot_rows.append(
                        spectrum[:, n * LANES : (n + 1) * LANES].reshape(-1, ROWS, LANES)
                    )
            a0, a2 = trade((shot_rows[0], shot_rows[2]), 4)
            a1, a3 = trade((shot_rows[1], shot_rows[3]), 4)
            devices = trade((a0, a1), 2) + trade((a2, a3), 2)
            for n, rows in enumerate(devices):
                out_buf[g, :, n, parity] = rows
        out_copy(g).start()
        return carry

    lax.fori_loop(0, steps, body, 0)
    for g in range(steps):
        out_copy(g).wait()


def dft(line_index, traces, radon_size, freq_size):
    shots, channels, _ = traces.shape
    devices = radon_size * freq_size
    step = LANES // channels * SPREAD
    steps = shots // step
    table = jnp.asarray(dft_tables(radon_size, freq_size))
    any_space = pl.BlockSpec(memory_space=pl.ANY)
    groups = (devices // SPREAD, SPREAD, BINS)
    out = pl.pallas_call(
        dft_kernel,
        in_specs=[pl.BlockSpec(memory_space=pltpu.SMEM), any_space, any_space],
        out_specs=any_space,
        out_shape=jax.ShapeDtypeStruct(groups + (steps * ROWS, LANES), jnp.float32),
        scratch_shapes=[
            pltpu.VMEM(traces.shape, jnp.float32),
            pltpu.VMEM((table.shape[0], 3 * HALF), table.dtype),
            pltpu.VMEM((steps,) + groups + (ROWS, LANES), jnp.float32),
        ]
        + [pltpu.VMEM((step * channels, 3 * HALF), jnp.bfloat16)] * BINS
        + [
            pltpu.SMEM((shots,), jnp.int32),
            pltpu.SemaphoreType.DMA((shots,)),
            pltpu.SemaphoreType.DMA,
            pltpu.SemaphoreType.DMA((steps,)),
        ],
        compiler_params=pltpu.CompilerParams(vmem_limit_bytes=60 * 2**20),
        cost_estimate=pl.CostEstimate(
            flops=3 * table.size * shots * channels,
            bytes_accessed=6 * traces.size,
            transcendentals=0,
        ),
    )(line_index, traces, table)
    return out.reshape(devices, BINS, steps * ROWS, LANES)


def weights_kernel(w_ref, out_ref):
    channels = w_ref.shape[2]
    for j in range(w_ref.shape[0]):
        for line in range(L):
            at = (pl.ds(j * channels, channels), pl.ds(line * P_SIZE, P_SIZE))
            hi, lo = split(w_ref[j, line])
            out_ref[0, at[0], at[1]] = hi
            out_ref[1, at[0], at[1]] = lo


def split_weights(weights):
    freq_size, _, channels, _ = weights.shape
    return pl.pallas_call(
        weights_kernel,
        out_shape=jax.ShapeDtypeStruct(
            (2, freq_size * channels, L * P_SIZE), jnp.bfloat16
        ),
        compiler_params=pltpu.CompilerParams(vmem_limit_bytes=32 * 2**20),
        cost_estimate=pl.CostEstimate(
            flops=10**11, bytes_accessed=8 * weights.size, transcendentals=0
        ),
    )(weights)


def panel_kernel(order, spots, freq_size, *refs):
    count = len(spots) // freq_size
    rec_refs, refs = refs[:count], refs[count:]
    (w_ref, src_ref, panel_ref, back_ref, out_ref), refs = refs[:5], refs[5:]
    a_refs, gathers = refs[: 2 * L], refs[2 * L :]
    step = pl.program_id(0)
    steps = pl.num_programs(0)
    _, bins, height, _ = rec_refs[0].shape
    channels = w_ref.shape[1] // freq_size
    tiles = height // ROWS // L
    halves = P_SIZE // LANES

    low = lax.broadcasted_iota(jnp.int32, (ROWS, LANES), 1) < channels
    rows = tiles * 2 * ROWS
    for line in range(L):
        a_hi, a_lo = a_refs[2 * line : 2 * line + 2]
        for parity in range(bins):
            for r in range(count):
                for t in range(tiles):
                    firsts, seconds = [], []
                    for j in range(0, freq_size, 2):
                        at = pl.ds((line * tiles + t) * ROWS, ROWS)
                        a, b = (
                            rec_refs[spot // freq_size][spot % freq_size, parity, at, :]
                            for spot in spots[r * freq_size + j : r * freq_size + j + 2]
                        )
                        firsts.append(jnp.where(low, a, pltpu.roll(b, channels, 1)))
                        seconds.append(jnp.where(low, pltpu.roll(a, channels, 1), b))
                    both = jnp.concatenate(
                        [jnp.concatenate(firsts, axis=1), jnp.concatenate(seconds, axis=1)],
                        axis=0,
                    )
                    at = pl.ds((parity * count + r) * rows + t * 2 * ROWS, 2 * ROWS)
                    a_hi[at, :], a_lo[at, :] = split(both)
        weights = w_ref[0, :, line * P_SIZE : (line + 1) * P_SIZE], w_ref[
            1, :, line * P_SIZE : (line + 1) * P_SIZE
        ]
        found = dot3((a_hi[...], a_lo[...]), weights)
        for parity in range(bins):
            for r in range(count):
                start = pl.multiple_of(((step * count + r) * L + line) * rows, rows)
                own = found[(parity * count + r) * rows : (parity * count + r + 1) * rows]
                for h in range(halves):
                    gathers[parity * halves + h][pl.ds(start, rows), :] = own[
                        :, h * LANES : (h + 1) * LANES
                    ]

    @pl.when(step == steps - 1)
    def _():
        shots = src_ref.shape[1]
        own = shots // out_ref.shape[0]
        source = split(src_ref[...])
        first = panel_ref[...] == 0
        for parity in range(bins):
            left, panels = ([], []), []
            for part in range(2):
                at = pl.ds(part, shots, stride=2)
                sorted_rows = jnp.concatenate(
                    split(
                        jnp.concatenate(
                            [gathers[parity * halves + h][at, :] for h in range(halves)], axis=1
                        )
                    ),
                    axis=1,
                )
                natural = [None] * len(order)
                for n in range(0, len(order), count):
                    mine = order[n : n + count]
                    back = jnp.concatenate([back_ref[r * own : (r + 1) * own] for r in mine])
                    found = jnp.dot(
                        back,
                        sorted_rows[n * own : (n + count) * own],
                        preferred_element_type=jnp.float32,
                    )
                    for i, r in enumerate(mine):
                        natural[r] = found[i * own : (i + 1) * own]
                natural = jnp.concatenate(natural, axis=0)
                pieces = natural[:, :P_SIZE], natural[:, P_SIZE:]
                panels.append(
                    split(dot3(source, [piece.astype(jnp.bfloat16) for piece in pieces]))
                )
                for k in range(K):
                    for kept, piece in zip(left, pieces):
                        chosen = jnp.where(first == (k == 0), piece, 0.0)
                        kept.append(chosen.astype(jnp.bfloat16))
            left = [jnp.concatenate(kept, axis=1) for kept in left]
            real, imag = panels
            rights = (
                [jnp.concatenate([real[n], -imag[n]], axis=0) for n in range(2)],
                [jnp.concatenate([imag[n], real[n]], axis=0) for n in range(2)],
            )
            for part in range(2):
                product = dot3(left, rights[part])
                for r in range(out_ref.shape[0]):
                    out_ref[r, parity, part] = product[r * own : (r + 1) * own]


def panel_products(received, weights, sources, panel_rows, back, radon_size):
    _, depth, columns = weights.shape
    freq_size = received.shape[0] // radon_size
    grid = GRID
    count = radon_size // grid
    order, spots, _ = exchange_order(radon_size, freq_size)
    shots = sources.shape[1]
    rows = shots // grid * 2
    out = (radon_size, BINS, 2, shots // radon_size, P_SIZE)
    return pl.pallas_call(
        functools.partial(panel_kernel, order, spots, freq_size),
        grid=(grid,),
        in_specs=[
            pl.BlockSpec(
                (freq_size,) + received.shape[1:], lambda r, n=n: (count * r + n, 0, 0, 0)
            )
            for n in range(count)
        ]
        + [
            pl.BlockSpec(weights.shape, lambda r: (0, 0, 0)),
            pl.BlockSpec(sources.shape, lambda r: (0, 0)),
            pl.BlockSpec((shots, 1), lambda r: (0, 0)),
            pl.BlockSpec(back.shape, lambda r: (0, 0)),
        ],
        out_specs=pl.BlockSpec(out, lambda r: (0, 0, 0, 0, 0)),
        out_shape=jax.ShapeDtypeStruct(out, jnp.float32),
        scratch_shapes=[pltpu.VMEM((BINS * rows // L, depth), jnp.bfloat16)] * (2 * L)
        + [pltpu.VMEM((grid * rows, LANES), jnp.float32)] * (BINS * P_SIZE // LANES),
        compiler_params=pltpu.CompilerParams(vmem_limit_bytes=48 * 2**20),
        cost_estimate=pl.CostEstimate(
            flops=6 * grid * BINS * rows * depth * P_SIZE,
            bytes_accessed=4 * received.size,
            transcendentals=0,
        ),
    )(*[received] * count, weights, sources, panel_rows, back)


def back_to_order(line_index, order):
    radon_size, count = len(order), len(order) // GRID
    lines = line_index.reshape(radon_size, -1)
    own = lines.shape[1]
    ranks = [jnp.cumsum((lines == line).astype(jnp.int32), axis=1) - 1 for line in range(L)]
    place = jnp.where(lines == 0, ranks[0], ranks[1] + own // L)
    offsets = np.array([own * (order.index(r) % count) for r in range(radon_size)], np.int32)
    place = (place + offsets[:, None]).reshape(-1)
    spots = jnp.arange(count * own, dtype=jnp.int32)
    return (place[:, None] == spots[None, :]).astype(jnp.bfloat16)


def shards(shot_traces, radon_weights, source_weights, line_index, panel_index):
    shot_rows = shot_traces.shape[0]
    freq_size = lax.axis_size("freq")
    radon_size = lax.axis_size("radon")

    weights = split_weights(lax.all_gather(radon_weights, "freq", axis=0))
    messages = dft(line_index, shot_traces, radon_size, freq_size)
    order, _, places = exchange_order(radon_size, freq_size)
    received = lax.all_to_all(
        messages, ("radon", "freq"), 0, 0, axis_index_groups=[places], tiled=True
    )

    onehot = panel_index[None, :] == jnp.arange(K, dtype=jnp.int32)[:, None]
    sources = jnp.where(onehot[:, None, :], source_weights.T[None], 0.0).reshape(K * P_SIZE, -1)

    back = back_to_order(line_index, order)
    products = panel_products(
        received, weights, sources, panel_index[:, None], back, radon_size
    )
    result = lax.all_to_all(products, "radon", 0, 0, tiled=True)
    return result.reshape(radon_size * BINS, 2, shot_rows, P_SIZE)


def solution(mesh):
    placed = (P("radon", "freq", None), P(None, "freq", None), P(), P(), P())
    return jax.shard_map(
        shards,
        mesh=mesh,
        in_specs=placed,
        out_specs=P("freq", None, "radon", None),
        check_vma=False,
    )
```

```python
import functools

import jax
import jax.numpy as jnp
import ml_dtypes
import numpy as np
from jax import lax
from jax.experimental import pallas as pl
from jax.experimental.pallas import tpu as pltpu
from jax.sharding import PartitionSpec as P

NT = 1024
NF = 256
P_SIZE = 256
L = 2
K = 2
HALF = NT // 2
LANES = 128
BINS = 2
ROWS = 8
SPREAD = ROWS // 2
AHEAD = 3
GRID = 2


def split(x):
    hi = x.astype(jnp.bfloat16)
    lo = (x - hi.astype(jnp.float32)).astype(jnp.bfloat16)
    return hi, lo


def dot3(a, b):
    dot = functools.partial(jnp.dot, preferred_element_type=jnp.float32)
    return dot(a[0], b[0]) + (dot(a[0], b[1]) + dot(a[1], b[0]))


def exchange_order(radon_size, freq_size):
    depth = radon_size // 2
    sources = [depth * y_lo + z for z in range(depth) for y_lo in range(2)]
    half = freq_size // 2
    devices = [
        (depth * y_lo + z) * freq_size + half * y_hi + n
        for z in range(depth)
        for y_hi in range(2)
        for y_lo in range(2)
        for n in range(half)
    ]
    count = radon_size // GRID
    spots = [devices.index(r * freq_size + j) for r in sources[:count] for j in range(freq_size)]
    return sources, spots, devices


def dft_tables(radon_size, freq_size):
    band = NF // freq_size
    order, _, places = exchange_order(radon_size, freq_size)
    device = np.array(places)
    first = band * (device % freq_size) + BINS * np.argsort(order)[device // freq_size]
    rows = []
    for parity in range(BINS):
        bins = first + parity
        phase = (bins[:, None] * np.arange(HALF)[None, :] % NT) * (2.0 * np.pi / NT)
        rows.append(np.stack([np.cos(phase), -np.sin(phase)], axis=1).reshape(-1, HALF))
    table = (np.concatenate(rows) * NT ** (-0.5)).astype(np.float32)
    hi = table.astype(ml_dtypes.bfloat16)
    lo = (table - hi.astype(np.float32)).astype(ml_dtypes.bfloat16)
    return np.concatenate([hi, lo], axis=1)


def trade(pieces, block):
    first, second = pieces
    row = lax.broadcasted_iota(jnp.int32, first.shape, 1)
    stay = lax.rem(lax.div(row, block), 2) == 0
    return (
        jnp.where(stay, first, pltpu.roll(second, block, 1)),
        jnp.where(stay, pltpu.roll(first, ROWS - block, 1), second),
    )


def dft_kernel(line_ref, x_hbm, table_hbm, out_hbm, x_buf, table, out_buf, *refs):
    folded, (order, x_sems, table_sem, out_sems) = refs[:-4], refs[-4:]
    steps = out_buf.shape[0]
    shots, channels, _ = x_buf.shape
    step = shots // steps
    count = table.shape[0] // BINS

    table_copy = pltpu.make_async_copy(table_hbm, table.at[:, : 2 * HALF], table_sem)
    table_copy.start()

    offset = lax.axis_index("radon") * shots

    def place(shot, counts):
        line = line_ref[offset + shot]
        order[jnp.where(line == 0, counts[0], counts[1])] = shot
        return (counts[0] + (1 - line), counts[1] + line)

    lax.fori_loop(0, shots, place, (jnp.int32(0), jnp.int32(shots // L)))

    def x_copy(n):
        return pltpu.make_async_copy(x_hbm.at[order[n]], x_buf.at[n], x_sems.at[n])

    def out_copy(g):
        return pltpu.make_async_copy(
            out_buf.at[g], out_hbm.at[:, :, :, pl.ds(g * ROWS, ROWS), :], out_sems.at[g]
        )

    for n in range(AHEAD * step):
        x_copy(n).start()
    table_copy.wait()
    table[:, 2 * HALF :] = table[:, :HALF]

    def body(g, carry):
        for n in range(step):
            x_copy(g * step + n).wait()

        @pl.when(g + AHEAD < steps)
        def _():
            for n in range(step):
                x_copy((g + AHEAD) * step + n).start()

        for sh in range(SPREAD):
            for i in range(2):
                shot = x_buf[g * step + SPREAD * i + sh]
                head, tail = shot[:, :HALF], shot[:, HALF:]
                at = pl.ds((sh * 2 + i) * channels, channels)
                for rows_ref, rows in zip(folded, (head + tail, head - tail)):
                    hi, lo = split(rows)
                    rows_ref[at, :HALF] = hi
                    rows_ref[at, HALF : 2 * HALF] = hi
                    rows_ref[at, 2 * HALF :] = lo
        for parity in range(BINS):
            shot_rows = []
            for half in range(2):
                spectrum = lax.dot_general(
                    table[parity * count : (parity + 1) * count],
                    folded[parity][half * 2 * LANES : (half + 1) * 2 * LANES],
                    (((1,), (1,)), ((), ())),
                    preferred_element_type=jnp.float32,
                )
                for n in range(2):
                    shot_rows.append(
                        spectrum[:, n * LANES : (n + 1) * LANES].reshape(-1, ROWS, LANES)
                    )
            a0, a2 = trade((shot_rows[0], shot_rows[2]), 4)
            a1, a3 = trade((shot_rows[1], shot_rows[3]), 4)
            devices = trade((a0, a1), 2) + trade((a2, a3), 2)
            for n, rows in enumerate(devices):
                out_buf[g, :, n, parity] = rows
        out_copy(g).start()
        return carry

    lax.fori_loop(0, steps, body, 0)
    for g in range(steps):
        out_copy(g).wait()


def dft(line_index, traces, radon_size, freq_size):
    shots, channels, _ = traces.shape
    devices = radon_size * freq_size
    step = LANES // channels * SPREAD
    steps = shots // step
    table = jnp.asarray(dft_tables(radon_size, freq_size))
    any_space = pl.BlockSpec(memory_space=pl.ANY)
    groups = (devices // SPREAD, SPREAD, BINS)
    out = pl.pallas_call(
        dft_kernel,
        in_specs=[pl.BlockSpec(memory_space=pltpu.SMEM), any_space, any_space],
        out_specs=any_space,
        out_shape=jax.ShapeDtypeStruct(groups + (steps * ROWS, LANES), jnp.float32),
        scratch_shapes=[
            pltpu.VMEM(traces.shape, jnp.float32),
            pltpu.VMEM((table.shape[0], 3 * HALF), table.dtype),
            pltpu.VMEM((steps,) + groups + (ROWS, LANES), jnp.float32),
        ]
        + [pltpu.VMEM((step * channels, 3 * HALF), jnp.bfloat16)] * BINS
        + [
            pltpu.SMEM((shots,), jnp.int32),
            pltpu.SemaphoreType.DMA((shots,)),
            pltpu.SemaphoreType.DMA,
            pltpu.SemaphoreType.DMA((steps,)),
        ],
        compiler_params=pltpu.CompilerParams(vmem_limit_bytes=60 * 2**20),
        cost_estimate=pl.CostEstimate(
            flops=3 * table.size * shots * channels,
            bytes_accessed=6 * traces.size,
            transcendentals=0,
        ),
    )(line_index, traces, table)
    return out.reshape(devices, BINS, steps * ROWS, LANES)


def weights_kernel(w_ref, out_ref):
    channels = w_ref.shape[2]
    for j in range(w_ref.shape[0]):
        for line in range(L):
            at = (pl.ds(j * channels, channels), pl.ds(line * P_SIZE, P_SIZE))
            hi, lo = split(w_ref[j, line])
            out_ref[0, at[0], at[1]] = hi
            out_ref[1, at[0], at[1]] = lo


def split_weights(weights):
    freq_size, _, channels, _ = weights.shape
    return pl.pallas_call(
        weights_kernel,
        out_shape=jax.ShapeDtypeStruct(
            (2, freq_size * channels, L * P_SIZE), jnp.bfloat16
        ),
        compiler_params=pltpu.CompilerParams(vmem_limit_bytes=32 * 2**20),
        cost_estimate=pl.CostEstimate(
            flops=10**11, bytes_accessed=8 * weights.size, transcendentals=0
        ),
    )(weights)


def panel_kernel(order, spots, freq_size, *refs):
    count = len(spots) // freq_size
    rec_refs, refs = refs[:count], refs[count:]
    (w_ref, src_ref, panel_ref, back_ref, out_ref), refs = refs[:5], refs[5:]
    a_refs, gathers = refs[: 2 * L], refs[2 * L :]
    step = pl.program_id(0)
    steps = pl.num_programs(0)
    _, bins, height, _ = rec_refs[0].shape
    channels = w_ref.shape[1] // freq_size
    tiles = height // ROWS // L
    halves = P_SIZE // LANES

    low = lax.broadcasted_iota(jnp.int32, (ROWS, LANES), 1) < channels
    rows = tiles * 2 * ROWS
    for line in range(L):
        a_hi, a_lo = a_refs[2 * line : 2 * line + 2]
        for parity in range(bins):
            for r in range(count):
                for t in range(tiles):
                    firsts, seconds = [], []
                    for j in range(0, freq_size, 2):
                        at = pl.ds((line * tiles + t) * ROWS, ROWS)
                        a, b = (
                            rec_refs[spot // freq_size][spot % freq_size, parity, at, :]
                            for spot in spots[r * freq_size + j : r * freq_size + j + 2]
                        )
                        firsts.append(jnp.where(low, a, pltpu.roll(b, channels, 1)))
                        seconds.append(jnp.where(low, pltpu.roll(a, channels, 1), b))
                    both = jnp.concatenate(
                        [jnp.concatenate(firsts, axis=1), jnp.concatenate(seconds, axis=1)],
                        axis=0,
                    )
                    at = pl.ds((parity * count + r) * rows + t * 2 * ROWS, 2 * ROWS)
                    a_hi[at, :], a_lo[at, :] = split(both)
        weights = w_ref[0, :, line * P_SIZE : (line + 1) * P_SIZE], w_ref[
            1, :, line * P_SIZE : (line + 1) * P_SIZE
        ]
        found = dot3((a_hi[...], a_lo[...]), weights)
        for parity in range(bins):
            for r in range(count):
                start = pl.multiple_of(((step * count + r) * L + line) * rows, rows)
                own = found[(parity * count + r) * rows : (parity * count + r + 1) * rows]
                for h in range(halves):
                    gathers[parity * halves + h][pl.ds(start, rows), :] = own[
                        :, h * LANES : (h + 1) * LANES
                    ]

    @pl.when(step == steps - 1)
    def _():
        shots = src_ref.shape[1]
        own = shots // out_ref.shape[0]
        source = split(src_ref[...])
        first = panel_ref[...] == 0
        for parity in range(bins):
            left, panels = ([], []), []
            for part in range(2):
                at = pl.ds(part, shots, stride=2)
                sorted_rows = jnp.concatenate(
                    split(
                        jnp.concatenate(
                            [gathers[parity * halves + h][at, :] for h in range(halves)], axis=1
                        )
                    ),
                    axis=1,
                )
                natural = [None] * len(order)
                for n in range(0, len(order), count):
                    mine = order[n : n + count]
                    back = jnp.concatenate([back_ref[r * own : (r + 1) * own] for r in mine])
                    found = jnp.dot(
                        back,
                        sorted_rows[n * own : (n + count) * own],
                        preferred_element_type=jnp.float32,
                    )
                    for i, r in enumerate(mine):
                        natural[r] = found[i * own : (i + 1) * own]
                natural = jnp.concatenate(natural, axis=0)
                pieces = natural[:, :P_SIZE], natural[:, P_SIZE:]
                panels.append(
                    split(dot3(source, [piece.astype(jnp.bfloat16) for piece in pieces]))
                )
                for k in range(K):
                    for kept, piece in zip(left, pieces):
                        chosen = jnp.where(first == (k == 0), piece, 0.0)
                        kept.append(chosen.astype(jnp.bfloat16))
            left = [jnp.concatenate(kept, axis=1) for kept in left]
            real, imag = panels
            rights = (
                [jnp.concatenate([real[n], -imag[n]], axis=0) for n in range(2)],
                [jnp.concatenate([imag[n], real[n]], axis=0) for n in range(2)],
            )
            for part in range(2):
                product = dot3(left, rights[part])
                for n, r in enumerate(order):
                    out_ref[n, parity, part] = product[r * own : (r + 1) * own]


def panel_products(received, weights, sources, panel_rows, back, radon_size):
    _, depth, columns = weights.shape
    freq_size = received.shape[0] // radon_size
    grid = GRID
    count = radon_size // grid
    order, spots, _ = exchange_order(radon_size, freq_size)
    shots = sources.shape[1]
    rows = shots // grid * 2
    out = (radon_size, BINS, 2, shots // radon_size, P_SIZE)
    return pl.pallas_call(
        functools.partial(panel_kernel, order, spots, freq_size),
        grid=(grid,),
        in_specs=[
            pl.BlockSpec(
                (freq_size,) + received.shape[1:], lambda r, n=n: (count * r + n, 0, 0, 0)
            )
            for n in range(count)
        ]
        + [
            pl.BlockSpec(weights.shape, lambda r: (0, 0, 0)),
            pl.BlockSpec(sources.shape, lambda r: (0, 0)),
            pl.BlockSpec((shots, 1), lambda r: (0, 0)),
            pl.BlockSpec(back.shape, lambda r: (0, 0)),
        ],
        out_specs=pl.BlockSpec(out, lambda r: (0, 0, 0, 0, 0)),
        out_shape=jax.ShapeDtypeStruct(out, jnp.float32),
        scratch_shapes=[pltpu.VMEM((BINS * rows // L, depth), jnp.bfloat16)] * (2 * L)
        + [pltpu.VMEM((grid * rows, LANES), jnp.float32)] * (BINS * P_SIZE // LANES),
        compiler_params=pltpu.CompilerParams(vmem_limit_bytes=48 * 2**20),
        cost_estimate=pl.CostEstimate(
            flops=6 * grid * BINS * rows * depth * P_SIZE,
            bytes_accessed=4 * received.size,
            transcendentals=0,
        ),
    )(*[received] * count, weights, sources, panel_rows, back)


def back_to_order(line_index, order):
    radon_size, count = len(order), len(order) // GRID
    lines = line_index.reshape(radon_size, -1)
    own = lines.shape[1]
    ranks = [jnp.cumsum((lines == line).astype(jnp.int32), axis=1) - 1 for line in range(L)]
    place = jnp.where(lines == 0, ranks[0], ranks[1] + own // L)
    offsets = np.array([own * (order.index(r) % count) for r in range(radon_size)], np.int32)
    place = (place + offsets[:, None]).reshape(-1)
    spots = jnp.arange(count * own, dtype=jnp.int32)
    return (place[:, None] == spots[None, :]).astype(jnp.bfloat16)


def shards(shot_traces, radon_weights, source_weights, line_index, panel_index):
    shot_rows = shot_traces.shape[0]
    freq_size = lax.axis_size("freq")
    radon_size = lax.axis_size("radon")

    weights = split_weights(lax.all_gather(radon_weights, "freq", axis=0))
    messages = dft(line_index, shot_traces, radon_size, freq_size)
    order, _, places = exchange_order(radon_size, freq_size)
    received = lax.all_to_all(
        messages, ("radon", "freq"), 0, 0, axis_index_groups=[places], tiled=True
    )

    onehot = panel_index[None, :] == jnp.arange(K, dtype=jnp.int32)[:, None]
    sources = jnp.where(onehot[:, None, :], source_weights.T[None], 0.0).reshape(K * P_SIZE, -1)

    back = back_to_order(line_index, order)
    products = panel_products(
        received, weights, sources, panel_index[:, None], back, radon_size
    )
    result = lax.all_to_all(products, "radon", 0, 0, axis_index_groups=[order], tiled=True)
    return result.reshape(radon_size * BINS, 2, shot_rows, P_SIZE)


def solution(mesh):
    placed = (P("radon", "freq", None), P(None, "freq", None), P(), P(), P())
    return jax.shard_map(
        shards,
        mesh=mesh,
        in_specs=placed,
        out_specs=P("freq", None, "radon", None),
        check_vma=False,
    )
```
